512 devices in a mesh: dom: 128 (over z, y, core), feat: 4 (over x).
Axes of the slice: x: 4, y: 8, z: 8, core: 2. Of those that a mesh axis runs over, the one named last changes fastest.
Arguments:
- grad_pre2: bfloat16 [262144, 512], P('dom', 'feat'), may hold values from -6 to 6
- aggregated2: bfloat16 [262144, 512], P('dom', 'feat'), may hold values from -6 to 6
- weight2: bfloat16 [512, 512], P('feat'), may hold values from -0.25 to 0.25
- pre1: bfloat16 [262144, 512], P('dom', 'feat'), may hold values from -6 to 6
- aggregated1: bfloat16 [262144, 512], P('dom', 'feat'), may hold values from -6 to 6
- weight1: bfloat16 [512, 512], P('feat'), may hold values from -0.25 to 0.25
- blocks: bfloat16 [2048, 6, 128, 128], P('dom'), may hold values from -0.21875 to 0.21875
- targets: int32 [2048, 6], P('dom'), may hold values from 0 to 2047, as said below
Outputs:
- grad_weight2: float32 [512, 512], P('feat')
- grad_weight1: float32 [512, 512], P('feat')
- grad_input: bfloat16 [262144, 512], P('dom', 'feat')
The draws below stay inside these ranges and needn't reach their ends.
Inputs may be any that keep to these rules, and one draw needn't show every extreme that they name: `targets`: partition p holds row tiles p * 16 to p * 16 + 15. Entry 0 of a row tile's list is the tile itself. Every other entry names a tile of partition p + o with -2 <= o <= 2: one of that partition's last 8 tiles if o < 0, one of its first 8 tiles if o > 0, any of its tiles if o = 0. The first row tile of every partition names partitions p - 2, p - 1, p + 1 and p + 2 wherever they exist; the number of blocks that name another partition varies from tile to tile.
All inputs are finite; a program needn't handle non-finite values.
Results may differ from the reference program's by a relative error of at most 0.015.
Values may be sent and summed in bfloat16 or wider, within the bound.
A program may use at most 64 MiB of HBM per device.

```python
import math
import jax
import jax.numpy as jnp
from jax import lax

D = 512
TILE = 128
BLOCKS = 6
REACH = 2
TD = 16
BT = 8
NTILES = 2048
NODES = 262144


def draw_targets(key, part):
    tile_index = jnp.arange(NTILES, dtype=jnp.int32)
    device = tile_index // TD
    local_idx = tile_index % TD
    domains = NTILES // TD
    extra = BLOCKS - 1
    key_offset = jax.random.fold_in(key, 11)
    key_bound = jax.random.fold_in(key, 23)
    key_any = jax.random.fold_in(key, 37)
    offset = jax.random.randint(key_offset, (NTILES, extra), -REACH, REACH + 1)
    forced_list = jnp.concatenate([-jnp.arange(REACH, 0, -1, dtype=jnp.int32), jnp.arange(1, REACH + 1, dtype=jnp.int32), jnp.zeros((extra - 2 * REACH,), jnp.int32)])
    column = jnp.arange(extra, dtype=jnp.int32)
    use_forced = (local_idx[:, None] == 0) & (column[None, :] < 2 * REACH)
    offset = jnp.where(use_forced, forced_list[None, :], offset)
    other_dev = device[:, None] + offset
    in_range = (other_dev >= 0) & (other_dev < domains)
    offset = jnp.where(in_range, offset, 0)
    edge_pick = jax.random.randint(key_bound, (NTILES, extra), 0, BT)
    any_pick = jax.random.randint(key_any, (NTILES, extra), 0, TD)
    within = jnp.where(offset < 0, TD - 1 - edge_pick, jnp.where(offset > 0, edge_pick, any_pick))
    chosen = (device[:, None] + offset) * TD + within
    return jnp.concatenate([tile_index[:, None], chosen], axis=1).astype(jnp.int32)


def block_levels(stream_key, dims, cuts, least, high):
    def one(dim, shards_of):
        draws = jax.random.uniform(jax.random.fold_in(jax.random.fold_in(stream_key, 6), dim), (shards_of,), jnp.float32, least / len(cuts), high / len(cuts))
        return jnp.repeat(jnp.exp(draws), dims[dim] // shards_of).reshape((-1,) + (1,) * (len(dims) - dim - 1))

    level = one(*cuts[0])
    for cut in cuts[1:]:
        level = level * one(*cut)
    return level


def gaussian(own_key, shape, spread, bound, split=(), kind=jnp.bfloat16):
    array = jax.random.normal(own_key, shape, jnp.float32) * spread
    if len(split) > 0:
        array = block_levels(own_key, shape, split, -0.22, 0.18) * array
    return jnp.clip(array, min=-bound, max=bound).astype(kind)


def setup_inputs(seed: int = 0) -> dict:
    seeds = jax.random.split(jax.random.key(seed), 9)
    grad_pre2 = gaussian(seeds[0], (NODES, D), 1.0, 6.0, ((0, 128), (1, 4)))
    aggregated2 = gaussian(seeds[1], (NODES, D), 1.0, 6.0, ((0, 128), (1, 4)))
    weight2 = gaussian(seeds[2], (D, D), D ** -0.5, 0.25, ((0, 4),))
    pre1 = gaussian(seeds[3], (NODES, D), 1.0, 6.0, ((0, 128), (1, 4)))
    aggregated1 = gaussian(seeds[4], (NODES, D), 1.0, 6.0, ((0, 128), (1, 4)))
    weight1 = gaussian(seeds[5], (D, D), D ** -0.5, 0.25, ((0, 4),))
    blocks = gaussian(seeds[6], (NTILES, BLOCKS, TILE, TILE), (BLOCKS * TILE) ** -0.5, 0.21875, ((0, 128),))
    targets = draw_targets(jax.random.fold_in(seeds[8], 71), 0)
    return dict(grad_pre2=grad_pre2, aggregated2=aggregated2, weight2=weight2, pre1=pre1, aggregated1=aggregated1, weight1=weight1, blocks=blocks, targets=targets)


def spread_tiles(blocks, targets, values):
    tile_total = targets.shape[0]
    tile_size = blocks.shape[2]
    col_count = values.shape[1]
    groups = tile_total // TD
    window = (2 * REACH + 1) * TD
    source_groups = values.reshape(groups, TD, tile_size, col_count)
    block_groups = blocks.reshape(groups, TD, BLOCKS, tile_size, tile_size)
    target_groups = targets.reshape(groups, TD * BLOCKS).astype(jnp.int32)
    group_ids = jnp.arange(groups, dtype=jnp.int32)
    own_mask = jnp.arange(window, dtype=jnp.int32) // TD == REACH

    def accumulate(totals, group_item):
        block_group, target_group, source_group, group_id = group_item
        products = jnp.einsum('rkij,rjc->rkic', block_group.astype(jnp.float32), source_group.astype(jnp.float32))
        base = (group_id - REACH) * TD
        relative = (target_group - base + 0 * REACH).astype(jnp.int32)
        local = jax.ops.segment_sum(products.reshape(TD * BLOCKS, tile_size, col_count), relative, num_segments=window)
        rounded = lax.optimization_barrier(local.astype(jnp.bfloat16)).astype(jnp.float32)
        local = jnp.where(own_mask[:, None, None], local, rounded)
        start = (group_id * TD).astype(jnp.int32)
        zero = jnp.zeros((), jnp.int32)
        current = lax.dynamic_slice(totals, (start, zero, zero), (window, tile_size, col_count))
        totals = lax.dynamic_update_slice(totals, current + local, (start, zero, zero))
        return (totals, None)
    start_total = jnp.zeros((tile_total + 2 * REACH * TD, tile_size, col_count), jnp.float32)
    totals, unused = lax.scan(accumulate, start_total, (block_groups, target_groups, source_groups, group_ids))
    totals = totals[REACH * TD:REACH * TD + tile_total]
    return totals.reshape(tile_total * tile_size, col_count)

def reference(grad_pre2, aggregated2, weight2, pre1, aggregated1, weight1, blocks, targets):
    grad_scale = 1.0 / math.sqrt(NODES)
    grad_weight2 = jnp.dot(aggregated2.T, grad_pre2, preferred_element_type=jnp.float32) * grad_scale
    grad_agg2 = jnp.dot(grad_pre2, weight2.T, preferred_element_type=jnp.float32).astype(jnp.bfloat16)
    grad_hidden1 = spread_tiles(blocks, targets, grad_agg2)
    grad_pre1 = jnp.where(pre1 > 0, grad_hidden1, 0.0).astype(jnp.bfloat16)
    grad_weight1 = jnp.dot(aggregated1.T, grad_pre1, preferred_element_type=jnp.float32) * grad_scale
    grad_agg1 = jnp.dot(grad_pre1, weight1.T, preferred_element_type=jnp.float32).astype(jnp.bfloat16)
    grad_input = spread_tiles(blocks, targets, grad_agg1).astype(jnp.bfloat16)
    return (grad_weight2, grad_weight1, grad_input)
```

```python
import functools
import math

import jax
import jax.numpy as jnp
from jax import lax
from jax.experimental import pallas as pl
from jax.experimental.pallas import tpu as pltpu
from jax.sharding import PartitionSpec as P

MESH = pl.DeviceIdType.MESH
BF = jnp.bfloat16
F32 = jnp.float32
IF, OF, IN, ON = 0, 1, 2, 3
H, B, N, A = 0, 1, 2, 3


def kernel(
    nz, ny, td, scale,
    gp2, agg2, w2, pre1, agg1, w1, blocks, ints, floats,
    gw2, gw1, gi,
    gath, blk, wv, pre, agg, aggt, prod, run, out, rec, giv, wacc, fin,
    w1s, w1r, wzs, wzr, wys, wyr, wgs, wgr, wcs, wcr,
    lsem, osem, gsend, grecv, ysend, yrecv, csend, crecv, zsend, zrecv, vsend, vrecv, tsend, trecv, c2send, c2recv,
):
    nb, tile, _ = blocks.shape
    bl = nb // td
    half = td // 2
    q = td // 4
    ch = q * tile
    yc, yt = 2, half // 2
    nx = lax.axis_size("feat")
    nd = lax.axis_size("dom")
    p = lax.axis_index("dom")
    x = lax.axis_index("feat")
    core = lax.rem(p, 2)
    y = lax.rem(p // 2, ny)
    z = p // (2 * ny)
    sig = 2 * core - 1

    def dom(step):
        return lax.rem(p + step + 2 * nd, nd)

    right = (p, lax.rem(x + 1, nx))
    left = (p, lax.rem(x + nx - 1, nx))
    partner, near, far, back = (dom(-sig), x), (dom(sig), x), (dom(2 * sig), x), (dom(-2 * sig), x)

    def zdev(k):
        return (k * (2 * ny) + y * 2 + core, x)

    def ydev(k):
        return (z * (2 * ny) + k * 2 + core, x)

    local = []

    def fetch(src, dst, i):
        cp = pltpu.make_async_copy(src, dst, lsem.at[i])
        cp.start()
        return cp

    def cols(k):
        return pl.ds(pl.multiple_of(k * tile, tile), tile)

    barrier = pltpu.get_barrier_semaphore()
    for dev in (left, right, partner, near, far, back):
        pl.semaphore_signal(barrier, inc=1, device_id=dev, device_id_type=MESH)

    def greet(k, _):
        pl.semaphore_signal(barrier, inc=1, device_id=zdev(lax.rem(z + k, nz)), device_id_type=MESH)
        return 0

    lax.fori_loop(1, nz, greet, 0)

    def greet_y(k, _):
        pl.semaphore_signal(barrier, inc=1, device_id=ydev(lax.rem(y + k, ny)), device_id_type=MESH)
        return 0

    lax.fori_loop(1, ny, greet_y, 0)

    own_cp = fetch(gp2, gath.at[0, :, cols(x)], 0)
    w2_cp = fetch(w2, wv.at[0], 1)
    agg2_cp = fetch(agg2, agg.at[0], 2)
    blk_cp = fetch(blocks, blk, 3)
    pre_cp = fetch(pre1, pre, 4)
    w1_cp = fetch(w1, wv.at[1], 5)
    agg1_cp = fetch(agg1, agg.at[1], 6)

    pl.semaphore_wait(barrier, 6 + nz - 1 + ny - 1)

    sends = []

    def remote(src, dst, ssem, rsem, dev):
        return pltpu.make_async_remote_copy(
            src_ref=src, dst_ref=dst, send_sem=ssem, recv_sem=rsem, device_id=dev, device_id_type=MESH
        )

    def send(*a):
        cp = remote(*a)
        cp.start()
        sends.append(cp)

    def first_tile(c):
        base = (1 - core) * half if c < 2 else core * half
        return base + (c % 2) * q

    def rows(c):
        return pl.ds(pl.multiple_of(first_tile(c) * tile, tile), ch)

    def gcopy(l, c, way, owner, dev):
        dst = gath.at[l, rows(c), cols(owner)]
        src = gp2.at[rows(c), :] if l == 0 and way < 2 else dst
        return src, dst, gsend.at[l, c, way], grecv.at[l, c, way], dev

    def send_own(l, c, way):
        send(*gcopy(l, c, way, x, right if way == 0 else left))

    def arrived(l, c, way):
        owner = lax.rem(x + (nx - 1, 1, 2)[way], nx)
        remote(*gcopy(l, c, way, owner, left)).wait_recv()

    def forward(l, c):
        if c % 2 == 0:
            arrived(l, c, 0)
            send(*gcopy(l, c, 2, left[1], right))
        else:
            arrived(l, c, 1)
            send(*gcopy(l, c, 2, right[1], left))

    def dense(l, c):
        arrived(l, c, 1 if c % 2 == 0 else 0)
        arrived(l, c, 2)

        def one(t, _):
            k = first_tile(c) + t
            g = gath[l, pl.ds(pl.multiple_of(k * tile, tile), tile), :]
            v = lax.dot_general(g, wv[l], (((1,), (1,)), ((), ())), preferred_element_type=F32).astype(BF)
            b = blk[pl.ds(k * bl, bl)].reshape(bl * tile, tile)
            prod[pl.ds(k * bl, bl)] = jnp.dot(b, v, preferred_element_type=F32).reshape(bl, tile, tile)
            return 0

        lax.fori_loop(0, q, one, 0)
        term = jnp.dot(aggt[l, c], gath[l, rows(c), :], preferred_element_type=F32)
        if c == 0:
            wacc[l] = term
        else:
            wacc[l] += term

    def transpose_agg(l):
        for c in range(4):
            aggt[l, c] = agg[l, rows(c), :].T

    def run_sums():
        def one(i, acc):
            acc = acc * floats[i] + prod[ints[i]]
            run[i] = acc
            return acc

        lax.fori_loop(0, nb, one, jnp.zeros((tile, tile), F32))

    def slot(s):
        return run[ints[nb + s]] * floats[nb + s]

    def ycopy(l, g, c, dev):
        at = pl.ds(c * yt, yt)
        return out.at[l, g, at], rec.at[l, g, at], ysend.at[l, g, c], yrecv.at[l, g, c], dev

    def emit(l, g, c, dev):
        def one(j, _):
            val = slot(g * half + c * yt + j)
            if g == ON:
                val = val + rec[l, H, c * yt + j].astype(F32)
            out[l, g, c * yt + j] = val.astype(BF)
            return 0

        if g == ON:
            remote(*ycopy(l, H, c, partner)).wait_recv()
        lax.fori_loop(0, yt, one, 0)
        send(*ycopy(l, g, c, dev))

    def spread(l):
        run_sums()
        for c in range(yc):
            emit(l, IF, c, partner)
        for c in range(yc):
            emit(l, OF, c, far)
        for c in range(yc):
            emit(l, IN, c, partner)
        for c in range(yc):
            emit(l, ON, c, near)

    def collect(l, c, put):
        groups = (B, N) if c < 2 else (A,)
        cc = c % 2
        for g in groups:
            remote(*ycopy(l, g, cc, partner)).wait_recv()

        def one(j, _):
            k = first_tile(c) + j
            val = slot(4 * half + k)
            for g in groups:
                val = val + rec[l, g, cc * yt + j].astype(F32)
            put(k, val)
            return 0

        lax.fori_loop(0, q, one, 0)

    hr = tile // 2
    rc = wzs.shape[1] // 2
    pr = hr // rc

    def piece(k):
        return pl.ds(pl.multiple_of((k // 2) * pr, pr), pr), pl.ds(pl.multiple_of(lax.rem(k, 2) * 256, 256), 256)

    def c1copy(l):
        return w1s.at[l], w1r.at[l], csend.at[l], crecv.at[l], partner

    def weight1(l):
        w1s[l] = (wacc[l, pl.ds(pl.multiple_of((1 - core) * hr, hr), hr), :] * scale).astype(BF)
        send(*c1copy(l))

    def others(n, me, make):
        def go(k, _):
            make(lax.rem(me + k, n)).start()
            return 0

        lax.fori_loop(1, n, go, 0)

    def all_recv(n, me, make):
        def go(k, _):
            make(lax.rem(me + k, n)).wait_recv()
            return 0

        lax.fori_loop(1, n, go, 0)

    def all_sent(n, me, make):
        def go(k, _):
            make(lax.rem(me + k, n)).wait_send()
            return 0

        lax.fori_loop(1, n, go, 0)

    def zout(l):
        return lambda k: remote(wzs.at[l, k], wzr.at[l, z], zsend.at[l, k], zrecv.at[l, z], zdev(k))

    def zin(l):
        return lambda k: remote(wzs.at[l, k], wzr.at[l, k], zsend.at[l, k], zrecv.at[l, k], zdev(k))

    def yout(l):
        return lambda k: remote(wys.at[l], wyr.at[l, y], vsend.at[l, k], vrecv.at[l, y], ydev(k))

    def yin(l):
        return lambda k: remote(wys.at[l], wyr.at[l, k], vsend.at[l, k], vrecv.at[l, k], ydev(k))

    def gout(l):
        return lambda k: remote(wgs.at[l], wgr.at[l, z], tsend.at[l, k], trecv.at[l, z], zdev(k))

    def gin(l):
        return lambda k: remote(wgs.at[l], wgr.at[l, k], tsend.at[l, k], trecv.at[l, k], zdev(k))

    def weight2(l):
        remote(*c1copy(l)).wait_recv()
        fin[l] = wacc[l, pl.ds(pl.multiple_of(core * hr, hr), hr), :] * scale + w1r[l].astype(F32)

        for k in range(nz):
            r, c = k // 2, k % 2
            wzs[l, k] = fin[l, r * pr:(r + 1) * pr, c * 256:(c + 1) * 256].astype(BF)
        others(nz, z, zout(l))

    def weight3(l):
        wzr[l, z] = wzs[l, z]
        all_recv(nz, z, zin(l))
        total = wzr[l, 0].astype(F32)
        for k in range(1, nz):
            total = total + wzr[l, k].astype(F32)
        wys[l] = total.astype(BF)
        others(ny, y, yout(l))

    def weight4(l):
        wyr[l, y] = wys[l]
        all_recv(ny, y, yin(l))
        total = wyr[l, 0].astype(F32)
        for k in range(1, ny):
            total = total + wyr[l, k].astype(F32)
        wgs[l] = total.astype(BF)
        others(nz, z, gout(l))

    def c2copy(l):
        return wcs.at[l], wcr.at[l], c2send.at[l], c2recv.at[l], partner

    def weight5(l):
        wgr[l, z] = wgs[l]
        all_recv(nz, z, gin(l))
        for k in range(nz):
            r, c = k // 2, k % 2
            wcs[l, r * pr:(r + 1) * pr, c * 256:(c + 1) * 256] = wgr[l, k]
        send(*c2copy(l))
        wacc[l, pl.ds(pl.multiple_of(core * hr, hr), hr), :] = wcs[l].astype(F32)

    outs = []

    def weight6(l):
        remote(*c2copy(l)).wait_recv()
        wacc[l, pl.ds(pl.multiple_of((1 - core) * hr, hr), hr), :] = wcr[l].astype(F32)
        cp = pltpu.make_async_copy(wacc.at[l], (gw2, gw1)[l], osem.at[l])
        cp.start()
        outs.append(cp)

    for c, d in ((0, 1), (2, 3), (1, 0), (3, 2)):
        send_own(0, c, 0)
        send_own(0, d, 1)
    agg2_cp.wait()
    transpose_agg(0)
    own_cp.wait()
    w2_cp.wait()
    forward(0, 0)
    forward(0, 1)
    blk_cp.wait()
    dense(0, 0)
    forward(0, 2)
    dense(0, 1)
    forward(0, 3)
    dense(0, 2)
    dense(0, 3)
    weight1(0)
    spread(0)
    weight2(0)
    pre_cp.wait()
    w1_cp.wait()

    def put_hidden(k, val):
        at = pl.ds(pl.multiple_of(k * tile, tile), tile)
        gath[1, at, cols(x)] = jnp.where(pre[at, :].astype(F32) > 0, val, 0.0).astype(BF)

    for c in range(4):
        collect(0, c, put_hidden)
        send_own(1, c, c % 2)
        send_own(1, c, 1 - c % 2)
        if c == 1:
            agg1_cp.wait()
            transpose_agg(1)
            forward(1, 0)
        if c == 2:
            forward(1, 1)
    weight3(0)
    dense(1, 0)
    forward(1, 2)
    weight4(0)
    dense(1, 1)
    forward(1, 3)
    weight5(0)
    dense(1, 2)
    weight6(0)
    dense(1, 3)
    weight1(1)
    spread(1)
    weight2(1)

    def put_input(k, val):
        giv[k] = val.astype(BF)

    for c in range(4):
        collect(1, c, put_input)
        at = pl.ds(first_tile(c), q)
        cp = pltpu.make_async_copy(giv.at[at], gi.at[at], osem.at[2 + c])
        cp.start()
        outs.append(cp)
        if c == 1:
            weight3(1)
        if c == 2:
            weight4(1)
    weight5(1)
    weight6(1)
    for cp in sends:
        cp.wait_send()
    for l in range(2):
        all_sent(nz, z, zin(l))
        all_sent(ny, y, yin(l))
        all_sent(nz, z, gin(l))
    for cp in outs:
        cp.wait()


def lists(targets, tile_count):
    p = lax.axis_index("dom")
    half = tile_count // 2
    sig = 2 * lax.rem(p, 2) - 1
    flat = targets.reshape(-1)
    nb = flat.shape[0]
    rel = flat - (p - 2) * tile_count
    off = (rel // tile_count - 2)
    at = rel % tile_count
    turned = off * sig
    group = jnp.where(turned == -2, IF, jnp.where(turned == 2, OF, jnp.where(turned == -1, IN, ON)))
    slot = jnp.where(off == 0, 4 * half + at, group * half + jnp.where(off < 0, at - half, at))
    idx = jnp.arange(nb, dtype=jnp.int32)
    key = slot * nb + idx
    rank = jnp.sum((key[None, :] < key[:, None]).astype(jnp.int32), axis=1)
    hit = rank[None, :] == idx[:, None]
    order = jnp.sum(jnp.where(hit, idx[None, :], 0), axis=1)
    prev = rank[None, :] == idx[:, None] - 1
    keep = jnp.sum(jnp.where(hit, slot[None, :], 0), axis=1) == jnp.sum(jnp.where(prev, slot[None, :] + 1, 0), axis=1) - 1
    slots = jnp.arange(4 * half + tile_count, dtype=jnp.int32)
    last = jnp.sum((slot[None, :] <= slots[:, None]).astype(jnp.int32), axis=1) - 1
    some = jnp.any(slot[None, :] == slots[:, None], axis=1)
    ints = jnp.concatenate([order, jnp.maximum(last, 0)])
    floats = jnp.concatenate([keep, some]).astype(F32)
    return ints, floats


def sizes(nd):
    chips = nd // 2
    nz = 1
    while nz * nz < chips:
        nz *= 2
    return nz, chips // nz


def shards(grad_pre2, aggregated2, weight2, pre1, aggregated1, weight1, blocks, targets):
    td, bl, tile, _ = blocks.shape
    nb, half, q = td * bl, td // 2, td // 4
    nd = lax.axis_size("dom")
    rows, d = grad_pre2.shape[0], weight2.shape[1]
    nz, ny = sizes(nd)
    scale = 1.0 / math.sqrt(rows * nd)
    ints, floats = lists(targets, td)
    pr = tile // 2 // max(1, nz // 2)
    hbm = pl.BlockSpec(memory_space=pl.ANY)
    smem = pl.BlockSpec(memory_space=pltpu.SMEM)
    dma = pltpu.SemaphoreType.DMA
    gw2, gw1, gi = pl.pallas_call(
        functools.partial(kernel, nz, ny, td, scale),
        out_shape=(
            jax.ShapeDtypeStruct((tile, d), F32),
            jax.ShapeDtypeStruct((tile, d), F32),
            jax.ShapeDtypeStruct((td, tile, tile), BF),
        ),
        in_specs=[hbm] * 7 + [smem] * 2,
        out_specs=(hbm, hbm, hbm),
        scratch_shapes=[
            pltpu.VMEM((2, rows, d), BF),
            pltpu.VMEM((nb, tile, tile), BF),
            pltpu.VMEM((2, tile, d), BF),
            pltpu.VMEM((rows, tile), BF),
            pltpu.VMEM((2, rows, tile), BF),
            pltpu.VMEM((2, 4, tile, rows // 4), BF),
            pltpu.VMEM((nb, tile, tile), F32),
            pltpu.VMEM((nb, tile, tile), F32),
            pltpu.VMEM((2, 4, half, tile, tile), BF),
            pltpu.VMEM((2, 4, half, tile, tile), BF),
            pltpu.VMEM((td, tile, tile), BF),
            pltpu.VMEM((2, tile, d), F32),
            pltpu.VMEM((2, tile // 2, d), F32),
            pltpu.VMEM((2, tile // 2, d), BF),
            pltpu.VMEM((2, tile // 2, d), BF),
            pltpu.VMEM((2, nz, pr, 256), BF),
            pltpu.VMEM((2, nz, pr, 256), BF),
            pltpu.VMEM((2, pr, 256), BF),
            pltpu.VMEM((2, ny, pr, 256), BF),
            pltpu.VMEM((2, pr, 256), BF),
            pltpu.VMEM((2, nz, pr, 256), BF),
            pltpu.VMEM((2, tile // 2, d), BF),
            pltpu.VMEM((2, tile // 2, d), BF),
            dma((7,)),
            dma((6,)),
            dma((2, 4, 3)),
            dma((2, 4, 3)),
            dma((2, 4, 2)),
            dma((2, 4, 2)),
            dma((2,)),
            dma((2,)),
            dma((2, nz)),
            dma((2, nz)),
            dma((2, ny)),
            dma((2, ny)),
            dma((2, nz)),
            dma((2, nz)),
            dma((2,)),
            dma((2,)),
        ],
        compiler_params=pltpu.CompilerParams(
            collective_id=0, has_side_effects=True, vmem_limit_bytes=48 * 1024 * 1024
        ),
    )(grad_pre2, aggregated2, weight2, pre1, aggregated1, weight1, blocks.reshape(nb, tile, tile), ints, floats)
    return gw2, gw1, gi.reshape(rows, tile)


def solution(mesh):
    placed = (
        P("dom", "feat"),
        P("dom", "feat"),
        P("feat", None),
        P("dom", "feat"),
        P("dom", "feat"),
        P("feat", None),
        P("dom", None, None, None),
        P("dom", None),
    )
    return jax.shard_map(
        shards,
        mesh=mesh,
        in_specs=placed,
        out_specs=(P("feat", None), P("feat", None), P("dom", "feat")),
        check_vma=False,
    )
```

```python
import functools
import math

import jax
import jax.numpy as jnp
from jax import lax
from jax.experimental import pallas as pl
from jax.experimental.pallas import tpu as pltpu
from jax.sharding import PartitionSpec as P

MESH = pl.DeviceIdType.MESH
BF = jnp.bfloat16
F32 = jnp.float32
IF, OF, IN, ON = 0, 1, 2, 3
H, B, N, A = 0, 1, 2, 3


def kernel(
    nz, ny, td, scale,
    gp2, agg2, w2, pre1, agg1, w1, blocks, tg,
    gw, gi,
    gath, blk, wv, pre, agg, aggt, prod, run, out, rec, giv, wacc, keys, slots, icols, fcols, ints, floats,
    w1s, w1r, wzs, wzr, wys, wyr, wgs, wgr, wcr,
    lsem, osem, gsend, grecv, ysend, yrecv, csend, crecv, zsend, zrecv, vsend, vrecv, tsend, trecv, c2send, c2recv,
):
    nb, tile, _ = blocks.shape
    bl = nb // td
    half = td // 2
    q = td // 4
    ch = q * tile
    yc, yt = 2, half // 2
    nx = lax.axis_size("feat")
    nd = lax.axis_size("dom")
    p = lax.axis_index("dom")
    x = lax.axis_index("feat")
    core = lax.rem(p, 2)
    y = lax.rem(p // 2, ny)
    z = p // (2 * ny)
    sig = 2 * core - 1

    def dom(step):
        return lax.rem(p + step + 2 * nd, nd)

    right = (p, lax.rem(x + 1, nx))
    left = (p, lax.rem(x + nx - 1, nx))
    partner, near, far, back = (dom(-sig), x), (dom(sig), x), (dom(2 * sig), x), (dom(-2 * sig), x)

    def zdev(k):
        return (k * (2 * ny) + y * 2 + core, x)

    def ydev(k):
        return (z * (2 * ny) + k * 2 + core, x)

    local = []

    def fetch(src, dst, i):
        cp = pltpu.make_async_copy(src, dst, lsem.at[i])
        cp.start()
        return cp

    def cols(k):
        return pl.ds(pl.multiple_of(k * tile, tile), tile)

    barrier = pltpu.get_barrier_semaphore()
    for dev in (left, right, partner, near, far, back):
        pl.semaphore_signal(barrier, inc=1, device_id=dev, device_id_type=MESH)

    def greet(k, _):
        pl.semaphore_signal(barrier, inc=1, device_id=zdev(lax.rem(z + k, nz)), device_id_type=MESH)
        return 0

    lax.fori_loop(1, nz, greet, 0)

    def greet_y(k, _):
        pl.semaphore_signal(barrier, inc=1, device_id=ydev(lax.rem(y + k, ny)), device_id_type=MESH)
        return 0

    lax.fori_loop(1, ny, greet_y, 0)

    own_cp = fetch(gp2, gath.at[0, :, cols(x)], 0)
    w2_cp = fetch(w2, wv.at[0], 1)
    agg2_cp = fetch(agg2, agg.at[0], 2)
    blk_cp = fetch(blocks, blk, 3)
    pre_cp = fetch(pre1, pre, 4)
    w1_cp = fetch(w1, wv.at[1], 5)
    agg1_cp = fetch(agg1, agg.at[1], 6)

    pl.semaphore_wait(barrier, 6 + nz - 1 + ny - 1)

    sends = []

    def remote(src, dst, ssem, rsem, dev):
        return pltpu.make_async_remote_copy(
            src_ref=src, dst_ref=dst, send_sem=ssem, recv_sem=rsem, device_id=dev, device_id_type=MESH
        )

    def send(*a):
        cp = remote(*a)
        cp.start()
        sends.append(cp)

    def first_tile(c):
        base = (1 - core) * half if c < 2 else core * half
        return base + (c % 2) * q

    def rows(c):
        return pl.ds(pl.multiple_of(first_tile(c) * tile, tile), ch)

    def gcopy(l, c, way, owner, dev):
        dst = gath.at[l, rows(c), cols(owner)]
        src = gp2.at[rows(c), :] if l == 0 and way < 2 else dst
        return src, dst, gsend.at[l, c, way], grecv.at[l, c, way], dev

    def send_own(l, c, way):
        send(*gcopy(l, c, way, x, right if way == 0 else left))

    def arrived(l, c, way):
        owner = lax.rem(x + (nx - 1, 1, 2)[way], nx)
        remote(*gcopy(l, c, way, owner, left)).wait_recv()

    def forward(l, c):
        if c % 2 == 0:
            arrived(l, c, 0)
            send(*gcopy(l, c, 2, left[1], right))
        else:
            arrived(l, c, 1)
            send(*gcopy(l, c, 2, right[1], left))

    def dense(l, c):
        arrived(l, c, 1 if c % 2 == 0 else 0)
        arrived(l, c, 2)

        def one(t, _):
            k = first_tile(c) + t
            g = gath[l, pl.ds(pl.multiple_of(k * tile, tile), tile), :]
            v = lax.dot_general(g, wv[l], (((1,), (1,)), ((), ())), preferred_element_type=F32).astype(BF)
            b = blk[pl.ds(k * bl, bl)].reshape(bl * tile, tile)
            prod[pl.ds(k * bl, bl)] = jnp.dot(b, v, preferred_element_type=F32).reshape(bl, tile, tile)
            return 0

        term = jnp.dot(aggt[l, c], gath[l, rows(c), :], preferred_element_type=F32)
        if c == 0:
            wacc[l] = term
        else:
            wacc[l] += term
        if c == 3 and l == 1:
            weight1(l)
        lax.fori_loop(0, q, one, 0, unroll=True)

    def transpose_agg(l):
        for c in range(4):
            aggt[l, c] = agg[l, rows(c), :].T

    def make_lists():
        lane = lax.broadcasted_iota(jnp.int32, (1, tile), 1)

        def one(i, row):
            rel = tg[i // bl, lax.rem(i, bl)] - (p - 2) * td
            off = lax.div(rel, td) - 2
            at = lax.rem(rel, td)
            turned = off * sig
            group = jnp.where(turned == -2, IF, jnp.where(turned == 2, OF, jnp.where(turned == -1, IN, ON)))
            to = jnp.where(off == 0, 4 * half + at, group * half + jnp.where(off < 0, at - half, at))
            key = to * nb + i
            slots[pl.ds(i, 1), :] = jnp.full((1, tile), to, jnp.int32)
            keys[pl.ds(i, 1), :] = jnp.full((1, tile), key, jnp.int32)
            return jnp.where(lane == i, key, row)

        row = lax.fori_loop(0, nb, one, jnp.full((1, tile), 1 << 20, jnp.int32))
        place = lax.broadcasted_iota(jnp.int32, (nb, tile), 1)
        block = lax.broadcasted_iota(jnp.int32, (nb, tile), 0)
        rank = jnp.sum((row < keys[...]).astype(jnp.int32), axis=1, keepdims=True)

        def add(mask, what):
            return jnp.sum(jnp.where(mask, what, 0), axis=0, keepdims=True)

        now, before = add(rank == place, slots[...]), add(rank == place - 1, slots[...])
        icols[0:1, :] = add(rank == place, block)
        icols[1:2, :] = jnp.maximum(add(slots[...] <= place, 1) - 1, 0)
        fcols[0:1, :] = jnp.where((now == before) & (lane > 0), 1.0, 0.0)
        fcols[1:2, :] = jnp.where(add(slots[...] == place, 1) > 0, 1.0, 0.0)
        icp = pltpu.make_async_copy(icols, ints, lsem.at[7])
        fcp = pltpu.make_async_copy(fcols, floats, lsem.at[8])
        icp.start()
        fcp.start()
        icp.wait()
        fcp.wait()

    def run_sums():
        def one(i, acc):
            acc = acc * floats[0, i] + prod[ints[0, i]]
            run[i] = acc
            return acc

        lax.fori_loop(0, nb, one, jnp.zeros((tile, tile), F32))

    def slot(s):
        return run[ints[1, s]] * floats[1, s]

    def ycopy(l, g, c, dev):
        at = pl.ds(c * yt, yt)
        return out.at[l, g, at], rec.at[l, g, at], ysend.at[l, g, c], yrecv.at[l, g, c], dev

    def emit(l, g, c, dev):
        def one(j, _):
            val = slot(g * half + c * yt + j)
            if g == ON:
                val = val + rec[l, H, c * yt + j].astype(F32)
            out[l, g, c * yt + j] = val.astype(BF)
            return 0

        if g == ON:
            remote(*ycopy(l, H, c, partner)).wait_recv()
        lax.fori_loop(0, yt, one, 0)
        send(*ycopy(l, g, c, dev))

    def spread(l, between):
        run_sums()
        for c in range(yc):
            emit(l, IF, c, partner)
        between(l)
        for c in range(yc):
            emit(l, OF, c, far)
        for c in range(yc):
            emit(l, ON, c, near)
        for c in range(yc):
            emit(l, IN, c, partner)

    def collect(l, c, put):
        groups = (B, N) if c < 2 else (A,)
        cc = c % 2
        for g in groups:
            remote(*ycopy(l, g, cc, partner)).wait_recv()

        def one(j, _):
            k = first_tile(c) + j
            val = slot(4 * half + k)
            for g in groups:
                val = val + rec[l, g, cc * yt + j].astype(F32)
            put(k, val)
            return 0

        lax.fori_loop(0, q, one, 0)

    hc = wacc.shape[2] // 2

    def half_of(l, h):
        at = pl.ds(pl.multiple_of(h * hc, hc), hc)
        return (wacc[l, :, at] * scale).reshape(wzs.shape[1:])

    def c1copy(l):
        return w1s.at[l], w1r.at[l], csend.at[l], crecv.at[l], partner

    def weight1(l):
        w1s[l] = half_of(l, 1 - core).astype(BF)
        send(*c1copy(l))

    def others(n, me, make):
        def go(k, _):
            make(lax.rem(me + k, n)).start()
            return 0

        lax.fori_loop(1, n, go, 0)

    def all_recv(n, me, make):
        def go(k, _):
            make(lax.rem(me + k, n)).wait_recv()
            return 0

        lax.fori_loop(1, n, go, 0)

    def all_sent(n, me, make):
        def go(k, _):
            make(lax.rem(me + k, n)).wait_send()
            return 0

        lax.fori_loop(1, n, go, 0)

    side, at_a, at_b = nz, (z, y), (y, z)

    def adev(l, k):
        return zdev(k) if l == 0 else ydev(k)

    def bdev(l, k):
        return ydev(k) if l == 0 else zdev(k)

    def zout(l):
        return lambda k: remote(wzs.at[l, k], wzr.at[l, at_a[l]], zsend.at[l, k], zrecv.at[l, at_a[l]], adev(l, k))

    def zin(l):
        return lambda k: remote(wzs.at[l, k], wzr.at[l, k], zsend.at[l, k], zrecv.at[l, k], adev(l, k))

    def yout(l):
        return lambda k: remote(wys.at[l], wyr.at[l, at_b[l]], vsend.at[l, k], vrecv.at[l, at_b[l]], bdev(l, k))

    def yin(l):
        return lambda k: remote(wys.at[l], wyr.at[l, k], vsend.at[l, k], vrecv.at[l, k], bdev(l, k))

    def gout(l):
        return lambda k: remote(wgs.at[l], wgr.at[l, at_a[l]], tsend.at[l, k], trecv.at[l, at_a[l]], adev(l, k))

    def gin(l):
        return lambda k: remote(wgs.at[l], wgr.at[l, k], tsend.at[l, k], trecv.at[l, k], adev(l, k))

    def weight2(l):
        remote(*c1copy(l)).wait_recv()
        wzs[l] = (half_of(l, core) + w1r[l].astype(F32)).astype(BF)
        others(side, at_a[l], zout(l))

    def weight3(l):
        wzr[l, at_a[l]] = wzs[l, at_a[l]]
        all_recv(side, at_a[l], zin(l))
        total = wzr[l, 0].astype(F32)
        for k in range(1, nz):
            total = total + wzr[l, k].astype(F32)
        wys[l] = total.astype(BF)
        others(side, at_b[l], yout(l))

    def weight4(l):
        wyr[l, at_b[l]] = wys[l]
        all_recv(side, at_b[l], yin(l))
        total = wyr[l, 0].astype(F32)
        for k in range(1, ny):
            total = total + wyr[l, k].astype(F32)
        wgs[l] = total.astype(BF)
        others(side, at_a[l], gout(l))

    def c2copy(l):
        return wgr.at[l], wcr.at[l], c2send.at[l], c2recv.at[l], partner

    outs = []

    def put_weight(l, h, src, i):
        at = pl.ds(pl.multiple_of(h * hc, hc), hc)
        cp = pltpu.make_async_copy(src.at[l], gw.at[l, :, :, at], osem.at[l, i])
        cp.start()
        outs.append(cp)

    def weight5(l):
        wgr[l, at_a[l]] = wgs[l]
        all_recv(side, at_a[l], gin(l))
        send(*c2copy(l))
        put_weight(l, core, wgr, 0)

    def weight6(l):
        remote(*c2copy(l)).wait_recv()
        put_weight(l, 1 - core, wcr, 1)

    for c, d in ((0, 1), (2, 3), (1, 0), (3, 2)):
        send_own(0, c, 0)
        send_own(0, d, 1)
    make_lists()
    agg2_cp.wait()
    transpose_agg(0)
    own_cp.wait()
    w2_cp.wait()
    forward(0, 0)
    forward(0, 1)
    blk_cp.wait()
    dense(0, 0)
    forward(0, 2)
    dense(0, 1)
    forward(0, 3)
    dense(0, 2)
    dense(0, 3)
    weight1(0)
    spread(0, lambda l: None)
    weight2(0)
    pre_cp.wait()
    w1_cp.wait()

    def put_hidden(k, val):
        at = pl.ds(pl.multiple_of(k * tile, tile), tile)
        gath[1, at, cols(x)] = jnp.where(pre[at, :].astype(F32) > 0, val, 0.0).astype(BF)

    for c in range(4):
        collect(0, c, put_hidden)
        send_own(1, c, c % 2)
        send_own(1, c, 1 - c % 2)
        if c == 1:
            agg1_cp.wait()
            transpose_agg(1)
            forward(1, 0)
        if c == 2:
            forward(1, 1)
    weight3(0)
    dense(1, 0)
    forward(1, 2)
    weight4(0)
    dense(1, 1)
    forward(1, 3)
    weight5(0)
    dense(1, 2)
    weight6(0)
    dense(1, 3)
    spread(1, weight2)
    weight3(1)

    def put_input(k, val):
        giv[k] = val.astype(BF)

    for c in range(4):
        collect(1, c, put_input)
        at = pl.ds(first_tile(c), q)
        cp = pltpu.make_async_copy(giv.at[at], gi.at[at], osem.at[2 + c // 2, c % 2])
        cp.start()
        outs.append(cp)
        if c == 1:
            weight4(1)
    weight5(1)
    weight6(1)
    for cp in sends:
        cp.wait_send()
    for l in range(2):
        all_sent(side, at_a[l], zin(l))
        all_sent(side, at_b[l], yin(l))
        all_sent(side, at_a[l], gin(l))
    for cp in outs:
        cp.wait()


def sizes(nd):
    chips = nd // 2
    nz = 1
    while nz * nz < chips:
        nz *= 2
    return nz, chips // nz


def shards(grad_pre2, aggregated2, weight2, pre1, aggregated1, weight1, blocks, targets):
    td, bl, tile, _ = blocks.shape
    nb, half, q = td * bl, td // 2, td // 4
    nd = lax.axis_size("dom")
    rows, d = grad_pre2.shape[0], weight2.shape[1]
    nz, ny = sizes(nd)
    scale = 1.0 / math.sqrt(rows * nd)
    pr = tile // nz
    hbm = pl.BlockSpec(memory_space=pltpu.HBM)
    anywhere = pl.BlockSpec(memory_space=pl.ANY)
    smem = pl.BlockSpec(memory_space=pltpu.SMEM)
    dma = pltpu.SemaphoreType.DMA
    gw, gi = pl.pallas_call(
        functools.partial(kernel, nz, ny, td, scale),
        out_shape=(
            jax.ShapeDtypeStruct((2, nz, pr, d), BF),
            jax.ShapeDtypeStruct((td, tile, tile), BF),
        ),
        in_specs=[hbm] * 7 + [smem],
        out_specs=(anywhere, anywhere),
        scratch_shapes=[
            pltpu.VMEM((2, rows, d), BF),
            pltpu.VMEM((nb, tile, tile), BF),
            pltpu.VMEM((2, tile, d), BF),
            pltpu.VMEM((rows, tile), BF),
            pltpu.VMEM((2, rows, tile), BF),
            pltpu.VMEM((2, 4, tile, rows // 4), BF),
            pltpu.VMEM((nb, tile, tile), F32),
            pltpu.VMEM((nb, tile, tile), F32),
            pltpu.VMEM((2, 4, half, tile, tile), BF),
            pltpu.VMEM((2, 4, half, tile, tile), BF),
            pltpu.VMEM((td, tile, tile), BF),
            pltpu.VMEM((2, tile, d), F32),
            pltpu.VMEM((nb, tile), jnp.int32),
            pltpu.VMEM((nb, tile), jnp.int32),
            pltpu.VMEM((8, tile), jnp.int32),
            pltpu.VMEM((8, tile), F32),
            pltpu.SMEM((8, tile), jnp.int32),
            pltpu.SMEM((8, tile), F32),
            pltpu.VMEM((2, nz, pr, d // 2), BF),
            pltpu.VMEM((2, nz, pr, d // 2), BF),
            pltpu.VMEM((2, nz, pr, d // 2), BF),
            pltpu.VMEM((2, nz, pr, d // 2), BF),
            pltpu.VMEM((2, pr, d // 2), BF),
            pltpu.VMEM((2, ny, pr, d // 2), BF),
            pltpu.VMEM((2, pr, d // 2), BF),
            pltpu.VMEM((2, nz, pr, d // 2), BF),
            pltpu.VMEM((2, nz, pr, d // 2), BF),
            dma((9,)),
            dma((4, 2)),
            dma((2, 4, 3)),
            dma((2, 4, 3)),
            dma((2, 4, 2)),
            dma((2, 4, 2)),
            dma((2,)),
            dma((2,)),
            dma((2, nz)),
            dma((2, nz)),
            dma((2, ny)),
            dma((2, ny)),
            dma((2, nz)),
            dma((2, nz)),
            dma((2,)),
            dma((2,)),
        ],
        compiler_params=pltpu.CompilerParams(
            collective_id=0, has_side_effects=True, vmem_limit_bytes=40 * 1024 * 1024
        ),
    )(*(pltpu.with_memory_space_constraint(a, pltpu.HBM) for a in (grad_pre2, aggregated2, weight2, pre1, aggregated1, weight1, blocks.reshape(nb, tile, tile))), targets)
    gw = gw.reshape(2, tile, d)
    return gw[0].astype(F32), gw[1].astype(F32), gi.reshape(rows, tile)


def solution(mesh):
    placed = (
        P("dom", "feat"),
        P("dom", "feat"),
        P("feat", None),
        P("dom", "feat"),
        P("dom", "feat"),
        P("feat", None),
        P("dom", None, None, None),
        P("dom", None),
    )
    return jax.shard_map(
        shards,
        mesh=mesh,
        in_specs=placed,
        out_specs=(P("feat", None), P("feat", None), P("dom", "feat")),
        check_vma=False,
    )
```

```python
import functools
import math

import jax
import jax.numpy as jnp
from jax import lax
from jax.experimental import pallas as pl
from jax.experimental.pallas import tpu as pltpu
from jax.sharding import PartitionSpec as P

MESH = pl.DeviceIdType.MESH
PARTS = 2
BF = jnp.bfloat16
F32 = jnp.float32
IF, OF, IN, ON = 0, 1, 2, 3
H, B, N, A = 0, 1, 2, 3


def kernel(
    nz, ny, td, scale,
    gp2, agg2, w2, pre1, agg1, w1, blocks, tg,
    gw, gi,
    gath, blk, wv, pre, agg, aggt, prod, run, out, rec, giv, wacc, keys, slots, icols, fcols, ints, floats,
    w1s, w1r, wzs, wzr, wys, wyr, wgs, wgr, wcr,
    lsem, osem, gisem, gsend, grecv, ysend, yrecv, csend, crecv, zsend, zrecv, vsend, vrecv, tsend, trecv, c2send, c2recv,
):
    nb, tile, _ = blocks.shape
    bl = nb // td
    half = td // 2
    q = half // PARTS
    ch = q * tile
    chunks = 2 * PARTS
    yc, yt = PARTS, q
    nx = lax.axis_size("feat")
    nd = lax.axis_size("dom")
    p = lax.axis_index("dom")
    x = lax.axis_index("feat")
    core = lax.rem(p, 2)
    y = lax.rem(p // 2, ny)
    z = p // (2 * ny)
    sig = 2 * core - 1

    def dom(step):
        return lax.rem(p + step + 2 * nd, nd)

    right = (p, lax.rem(x + 1, nx))
    left = (p, lax.rem(x + nx - 1, nx))
    partner, near, far, back = (dom(-sig), x), (dom(sig), x), (dom(2 * sig), x), (dom(-2 * sig), x)

    def zdev(k):
        return (k * (2 * ny) + y * 2 + core, x)

    def ydev(k):
        return (z * (2 * ny) + k * 2 + core, x)

    local = []

    def fetch(src, dst, i):
        cp = pltpu.make_async_copy(src, dst, lsem.at[i])
        cp.start()
        return cp

    def cols(k):
        return pl.ds(pl.multiple_of(k * tile, tile), tile)

    barrier = pltpu.get_barrier_semaphore()
    for dev in (left, right, partner, near, far, back):
        pl.semaphore_signal(barrier, inc=1, device_id=dev, device_id_type=MESH)

    def greet(k, _):
        pl.semaphore_signal(barrier, inc=1, device_id=zdev(lax.rem(z + k, nz)), device_id_type=MESH)
        return 0

    lax.fori_loop(1, nz, greet, 0)

    def greet_y(k, _):
        pl.semaphore_signal(barrier, inc=1, device_id=ydev(lax.rem(y + k, ny)), device_id_type=MESH)
        return 0

    lax.fori_loop(1, ny, greet_y, 0)

    own_cp = fetch(gp2, gath.at[0, :, cols(x)], 0)
    w2_cp = fetch(w2, wv.at[0], 1)
    agg2_cp = fetch(agg2, agg.at[0], 2)
    blk_cp = fetch(blocks, blk, 3)
    pre_cp = fetch(pre1, pre, 4)
    w1_cp = fetch(w1, wv.at[1], 5)
    agg1_cp = fetch(agg1, agg.at[1], 6)

    pl.semaphore_wait(barrier, 6 + nz - 1 + ny - 1)

    sends = []

    def remote(src, dst, ssem, rsem, dev):
        return pltpu.make_async_remote_copy(
            src_ref=src, dst_ref=dst, send_sem=ssem, recv_sem=rsem, device_id=dev, device_id_type=MESH
        )

    def send(*a):
        cp = remote(*a)
        cp.start()
        sends.append(cp)

    def first_tile(c):
        base = (1 - core) * half if c < PARTS else core * half
        return base + (c % PARTS) * q

    def rows(c):
        return pl.ds(pl.multiple_of(first_tile(c) * tile, tile), ch)

    def gcopy(l, c, way, owner, dev):
        dst = gath.at[l, rows(c), cols(owner)]
        src = gp2.at[rows(c), :] if l == 0 and way < 2 else dst
        return src, dst, gsend.at[l, c, way], grecv.at[l, c, way], dev

    def send_own(l, c, way):
        send(*gcopy(l, c, way, x, right if way == 0 else left))

    def arrived(l, c, way):
        owner = lax.rem(x + (nx - 1, 1, 2)[way], nx)
        remote(*gcopy(l, c, way, owner, left)).wait_recv()

    def forward(l, c):
        if c % 2 == 0:
            arrived(l, c, 0)
            send(*gcopy(l, c, 2, left[1], right))
        else:
            arrived(l, c, 1)
            send(*gcopy(l, c, 2, right[1], left))

    def dense(l, c):
        arrived(l, c, 1 if c % 2 == 0 else 0)
        arrived(l, c, 2)

        def one(t, _):
            k = first_tile(c) + t
            g = gath[l, pl.ds(pl.multiple_of(k * tile, tile), tile), :]
            v = lax.dot_general(g, wv[l], (((1,), (1,)), ((), ())), preferred_element_type=F32).astype(BF)
            b = blk[pl.ds(k * bl, bl)].reshape(bl * tile, tile)
            prod[pl.ds(k * bl, bl)] = jnp.dot(b, v, preferred_element_type=F32).reshape(bl, tile, tile)
            return 0

        term = jnp.dot(aggt[l, c], gath[l, rows(c), :], preferred_element_type=F32)
        if c == 0:
            wacc[l] = term
        else:
            wacc[l] += term
        if c == chunks - 1 and l == 1:
            weight1(l)
        lax.fori_loop(0, q, one, 0, unroll=True)

    def transpose_agg(l):
        for c in range(chunks):
            aggt[l, c] = agg[l, rows(c), :].T

    def make_lists():
        lane = lax.broadcasted_iota(jnp.int32, (1, tile), 1)

        def one(i, row):
            rel = tg[i // bl, lax.rem(i, bl)] - (p - 2) * td
            off = lax.div(rel, td) - 2
            at = lax.rem(rel, td)
            turned = off * sig
            group = jnp.where(turned == -2, IF, jnp.where(turned == 2, OF, jnp.where(turned == -1, IN, ON)))
            to = jnp.where(off == 0, 4 * half + at, group * half + jnp.where(off < 0, at - half, at))
            key = to * nb + i
            slots[pl.ds(i, 1), :] = jnp.full((1, tile), to, jnp.int32)
            keys[pl.ds(i, 1), :] = jnp.full((1, tile), key, jnp.int32)
            return jnp.where(lane == i, key, row)

        row = lax.fori_loop(0, nb, one, jnp.full((1, tile), 1 << 20, jnp.int32))
        place = lax.broadcasted_iota(jnp.int32, (nb, tile), 1)
        block = lax.broadcasted_iota(jnp.int32, (nb, tile), 0)
        rank = jnp.sum((row < keys[...]).astype(jnp.int32), axis=1, keepdims=True)

        def add(mask, what):
            return jnp.sum(jnp.where(mask, what, 0), axis=0, keepdims=True)

        now, before = add(rank == place, slots[...]), add(rank == place - 1, slots[...])
        icols[0:1, :] = add(rank == place, block)
        icols[1:2, :] = jnp.maximum(add(slots[...] <= place, 1) - 1, 0)
        fcols[0:1, :] = jnp.where((now == before) & (lane > 0), 1.0, 0.0)
        fcols[1:2, :] = jnp.where(add(slots[...] == place, 1) > 0, 1.0, 0.0)
        icp = pltpu.make_async_copy(icols, ints, lsem.at[7])
        fcp = pltpu.make_async_copy(fcols, floats, lsem.at[8])
        icp.start()
        fcp.start()
        icp.wait()
        fcp.wait()

    def run_sums():
        def one(i, acc):
            acc = acc * floats[0, i] + prod[ints[0, i]]
            run[i] = acc
            return acc

        lax.fori_loop(0, nb, one, jnp.zeros((tile, tile), F32))

    def slot(s):
        return run[ints[1, s]] * floats[1, s]

    def ycopy(l, g, c, dev):
        at = pl.ds(c * yt, yt)
        return out.at[l, g, at], rec.at[l, g, at], ysend.at[l, g, c], yrecv.at[l, g, c], dev

    def emit(l, g, c, dev):
        def one(j, _):
            val = slot(g * half + c * yt + j)
            if g == ON:
                val = val + rec[l, H, c * yt + j].astype(F32)
            out[l, g, c * yt + j] = val.astype(BF)
            return 0

        if g == ON:
            remote(*ycopy(l, H, c, partner)).wait_recv()
        lax.fori_loop(0, yt, one, 0)
        send(*ycopy(l, g, c, dev))

    def spread(l, between):
        run_sums()
        for c in range(yc):
            emit(l, IF, c, partner)
        between(l)
        for c in range(yc):
            emit(l, OF, c, far)
        for c in range(yc):
            emit(l, ON, c, near)
        for c in range(yc):
            emit(l, IN, c, partner)

    def collect(l, c, put):
        groups = (B, N) if c < PARTS else (A,)
        cc = c % PARTS
        for g in groups:
            remote(*ycopy(l, g, cc, partner)).wait_recv()

        def one(j, _):
            k = first_tile(c) + j
            val = slot(4 * half + k)
            for g in groups:
                val = val + rec[l, g, cc * yt + j].astype(F32)
            put(k, val)
            return 0

        lax.fori_loop(0, q, one, 0)

    hc = wacc.shape[2] // 2

    def half_of(l, h):
        at = pl.ds(pl.multiple_of(h * hc, hc), hc)
        return (wacc[l, :, at] * scale).reshape(wzs.shape[1:])

    def c1copy(l):
        return w1s.at[l], w1r.at[l], csend.at[l], crecv.at[l], partner

    def weight1(l):
        w1s[l] = half_of(l, 1 - core).astype(BF)
        send(*c1copy(l))

    def others(n, me, make):
        def go(k, _):
            make(lax.rem(me + k, n)).start()
            return 0

        lax.fori_loop(1, n, go, 0)

    def all_recv(n, me, make):
        def go(k, _):
            make(lax.rem(me + k, n)).wait_recv()
            return 0

        lax.fori_loop(1, n, go, 0)

    def all_sent(n, me, make):
        def go(k, _):
            make(lax.rem(me + k, n)).wait_send()
            return 0

        lax.fori_loop(1, n, go, 0)

    side, at_a, at_b = nz, (z, y), (y, z)

    def adev(l, k):
        return zdev(k) if l == 0 else ydev(k)

    def bdev(l, k):
        return ydev(k) if l == 0 else zdev(k)

    def zout(l):
        return lambda k: remote(wzs.at[l, k], wzr.at[l, at_a[l]], zsend.at[l, k], zrecv.at[l, at_a[l]], adev(l, k))

    def zin(l):
        return lambda k: remote(wzs.at[l, k], wzr.at[l, k], zsend.at[l, k], zrecv.at[l, k], adev(l, k))

    def yout(l):
        return lambda k: remote(wys.at[l], wyr.at[l, at_b[l]], vsend.at[l, k], vrecv.at[l, at_b[l]], bdev(l, k))

    def yin(l):
        return lambda k: remote(wys.at[l], wyr.at[l, k], vsend.at[l, k], vrecv.at[l, k], bdev(l, k))

    def gout(l):
        return lambda k: remote(wgs.at[l], wgr.at[l, at_a[l]], tsend.at[l, k], trecv.at[l, at_a[l]], adev(l, k))

    def gin(l):
        return lambda k: remote(wgs.at[l], wgr.at[l, k], tsend.at[l, k], trecv.at[l, k], adev(l, k))

    def weight2(l):
        remote(*c1copy(l)).wait_recv()
        wzs[l] = (half_of(l, core) + w1r[l].astype(F32)).astype(BF)
        others(side, at_a[l], zout(l))

    def weight3(l):
        wzr[l, at_a[l]] = wzs[l, at_a[l]]
        all_recv(side, at_a[l], zin(l))
        total = wzr[l, 0].astype(F32)
        for k in range(1, nz):
            total = total + wzr[l, k].astype(F32)
        wys[l] = total.astype(BF)
        others(side, at_b[l], yout(l))

    def weight4(l):
        wyr[l, at_b[l]] = wys[l]
        all_recv(side, at_b[l], yin(l))
        total = wyr[l, 0].astype(F32)
        for k in range(1, ny):
            total = total + wyr[l, k].astype(F32)
        wgs[l] = total.astype(BF)
        others(side, at_a[l], gout(l))

    def c2copy(l):
        return wgr.at[l], wcr.at[l], c2send.at[l], c2recv.at[l], partner

    outs = []

    def put_weight(l, h, src, i):
        at = pl.ds(pl.multiple_of(h * hc, hc), hc)
        cp = pltpu.make_async_copy(src.at[l], gw.at[l, :, :, at], osem.at[l, i])
        cp.start()
        outs.append(cp)

    def weight5(l):
        wgr[l, at_a[l]] = wgs[l]
        all_recv(side, at_a[l], gin(l))
        send(*c2copy(l))
        put_weight(l, core, wgr, 0)

    def weight6(l):
        remote(*c2copy(l)).wait_recv()
        put_weight(l, 1 - core, wcr, 1)

    evens, odds = list(range(0, chunks, 2)), list(range(1, chunks, 2))
    for c, d in zip(evens + odds, odds + evens):
        send_own(0, c, 0)
        send_own(0, d, 1)
    make_lists()
    agg2_cp.wait()
    transpose_agg(0)
    own_cp.wait()
    w2_cp.wait()
    blk_cp.wait()
    for c in range(chunks):
        forward(0, c)
    for c in range(chunks):
        dense(0, c)
    weight1(0)
    spread(0, lambda l: None)
    weight2(0)
    agg1_cp.wait()
    transpose_agg(1)
    pre_cp.wait()
    w1_cp.wait()

    def put_hidden(k, val):
        at = pl.ds(pl.multiple_of(k * tile, tile), tile)
        gath[1, at, cols(x)] = jnp.where(pre[at, :].astype(F32) > 0, val, 0.0).astype(BF)

    for c in range(chunks):
        collect(0, c, put_hidden)
        send_own(1, c, c % 2)
        send_own(1, c, 1 - c % 2)
    weight3(0)
    for c in range(chunks):
        forward(1, c)
    weight4(0)
    for c in range(chunks):
        dense(1, c)
    weight2(1)
    spread(1, lambda l: None)
    weight3(1)
    weight5(0)

    def put_input(k, val):
        giv[k] = val.astype(BF)

    for c in range(chunks):
        collect(1, c, put_input)
        at = pl.ds(first_tile(c), q)
        cp = pltpu.make_async_copy(giv.at[at], gi.at[at], gisem.at[c])
        cp.start()
        outs.append(cp)
        if c == PARTS - 1:
            weight4(1)
    weight6(0)
    weight5(1)
    weight6(1)
    for cp in sends:
        cp.wait_send()
    for l in range(2):
        all_sent(side, at_a[l], zin(l))
        all_sent(side, at_b[l], yin(l))
        all_sent(side, at_a[l], gin(l))
    for cp in outs:
        cp.wait()


def sizes(nd):
    chips = nd // 2
    nz = 1
    while nz * nz < chips:
        nz *= 2
    return nz, chips // nz


def shards(grad_pre2, aggregated2, weight2, pre1, aggregated1, weight1, blocks, targets):
    td, bl, tile, _ = blocks.shape
    nb, half = td * bl, td // 2
    nd = lax.axis_size("dom")
    rows, d = grad_pre2.shape[0], weight2.shape[1]
    nz, ny = sizes(nd)
    scale = 1.0 / math.sqrt(rows * nd)
    pr = tile // nz
    hbm = pl.BlockSpec(memory_space=pltpu.HBM)
    anywhere = pl.BlockSpec(memory_space=pl.ANY)
    smem = pl.BlockSpec(memory_space=pltpu.SMEM)
    dma = pltpu.SemaphoreType.DMA
    gw, gi = pl.pallas_call(
        functools.partial(kernel, nz, ny, td, scale),
        out_shape=(
            jax.ShapeDtypeStruct((2, nz, pr, d), BF),
            jax.ShapeDtypeStruct((td, tile, tile), BF),
        ),
        in_specs=[hbm] * 7 + [smem],
        out_specs=(anywhere, anywhere),
        scratch_shapes=[
            pltpu.VMEM((2, rows, d), BF),
            pltpu.VMEM((nb, tile, tile), BF),
            pltpu.VMEM((2, tile, d), BF),
            pltpu.VMEM((rows, tile), BF),
            pltpu.VMEM((2, rows, tile), BF),
            pltpu.VMEM((2, 2 * PARTS, tile, rows // (2 * PARTS)), BF),
            pltpu.VMEM((nb, tile, tile), F32),
            pltpu.VMEM((nb, tile, tile), F32),
            pltpu.VMEM((2, 4, half, tile, tile), BF),
            pltpu.VMEM((2, 4, half, tile, tile), BF),
            pltpu.VMEM((td, tile, tile), BF),
            pltpu.VMEM((2, tile, d), F32),
            pltpu.VMEM((nb, tile), jnp.int32),
            pltpu.VMEM((nb, tile), jnp.int32),
            pltpu.VMEM((8, tile), jnp.int32),
            pltpu.VMEM((8, tile), F32),
            pltpu.SMEM((8, tile), jnp.int32),
            pltpu.SMEM((8, tile), F32),
            pltpu.VMEM((2, nz, pr, d // 2), BF),
            pltpu.VMEM((2, nz, pr, d // 2), BF),
            pltpu.VMEM((2, nz, pr, d // 2), BF),
            pltpu.VMEM((2, nz, pr, d // 2), BF),
            pltpu.VMEM((2, pr, d // 2), BF),
            pltpu.VMEM((2, ny, pr, d // 2), BF),
            pltpu.VMEM((2, pr, d // 2), BF),
            pltpu.VMEM((2, nz, pr, d // 2), BF),
            pltpu.VMEM((2, nz, pr, d // 2), BF),
            dma((9,)),
            dma((2, 2)),
            dma((2 * PARTS,)),
            dma((2, 2 * PARTS, 3)),
            dma((2, 2 * PARTS, 3)),
            dma((2, 4, PARTS)),
            dma((2, 4, PARTS)),
            dma((2,)),
            dma((2,)),
            dma((2, nz)),
            dma((2, nz)),
            dma((2, ny)),
            dma((2, ny)),
            dma((2, nz)),
            dma((2, nz)),
            dma((2,)),
            dma((2,)),
        ],
        compiler_params=pltpu.CompilerParams(
            collective_id=0, has_side_effects=True, vmem_limit_bytes=40 * 1024 * 1024
        ),
    )(*(pltpu.with_memory_space_constraint(a, pltpu.HBM) for a in (grad_pre2, aggregated2, weight2, pre1, aggregated1, weight1, blocks.reshape(nb, tile, tile))), targets)
    gw = gw.reshape(2, tile, d)
    return gw[0].astype(F32), gw[1].astype(F32), gi.reshape(rows, tile)


def solution(mesh):
    placed = (
        P("dom", "feat"),
        P("dom", "feat"),
        P("feat", None),
        P("dom", "feat"),
        P("dom", "feat"),
        P("feat", None),
        P("dom", None, None, None),
        P("dom", None),
    )
    return jax.shard_map(
        shards,
        mesh=mesh,
        in_specs=placed,
        out_specs=(P("feat", None), P("feat", None), P("dom", "feat")),
        check_vma=False,
    )
```

```python
import functools
import math

import jax
import jax.numpy as jnp
from jax import lax
from jax.experimental import pallas as pl
from jax.experimental.pallas import tpu as pltpu
from jax.sharding import PartitionSpec as P

MESH = pl.DeviceIdType.MESH
PARTS = 4
BF = jnp.bfloat16
F32 = jnp.float32
IF, OF, IN, ON = 0, 1, 2, 3
H, B, N, A = 0, 1, 2, 3


def kernel(
    nz, ny, td, scale,
    gp2, agg2, w2, pre1, agg1, w1, blocks, targets,
    gw, gi,
    gath, blk, wv, pre, agg, aggt, prod, run, out, rec, giv, wacc, keys, slots, icols, fcols, tg, ints, floats,
    w1s, w1r, wzs, wzr, wys, wyr, wgs, wgr, wcr,
    lsem, osem, gisem, gsend, grecv, ysend, yrecv, csend, crecv, zsend, zrecv, vsend, vrecv, tsend, trecv, c2send, c2recv,
):
    nb, tile, _ = blocks.shape
    bl = nb // td
    half = td // 2
    q = half // PARTS
    ch = q * tile
    chunks = 2 * PARTS
    yc, yt = PARTS, q
    nx = lax.axis_size("feat")
    nd = lax.axis_size("dom")
    p = lax.axis_index("dom")
    x = lax.axis_index("feat")
    core = lax.rem(p, 2)
    y = lax.rem(p // 2, ny)
    z = p // (2 * ny)
    sig = 2 * core - 1

    def dom(step):
        return lax.rem(p + step + 2 * nd, nd)

    right = (p, lax.rem(x + 1, nx))
    left = (p, lax.rem(x + nx - 1, nx))
    partner, near, far, back = (dom(-sig), x), (dom(sig), x), (dom(2 * sig), x), (dom(-2 * sig), x)

    def zdev(k):
        return (k * (2 * ny) + y * 2 + core, x)

    def ydev(k):
        return (z * (2 * ny) + k * 2 + core, x)

    local = []

    def fetch(src, dst, i):
        cp = pltpu.make_async_copy(src, dst, lsem.at[i])
        cp.start()
        return cp

    def cols(k):
        return pl.ds(pl.multiple_of(k * tile, tile), tile)

    barrier = pltpu.get_barrier_semaphore()
    for dev in (left, right, partner, near, far, back):
        pl.semaphore_signal(barrier, inc=1, device_id=dev, device_id_type=MESH)

    def greet(k, _):
        pl.semaphore_signal(barrier, inc=1, device_id=zdev(lax.rem(z + k, nz)), device_id_type=MESH)
        return 0

    lax.fori_loop(1, nz, greet, 0)

    def greet_y(k, _):
        pl.semaphore_signal(barrier, inc=1, device_id=ydev(lax.rem(y + k, ny)), device_id_type=MESH)
        return 0

    lax.fori_loop(1, ny, greet_y, 0)

    tg_cp = fetch(targets, tg, 9)
    own_cp = fetch(gp2, gath.at[0, :, cols(x)], 0)
    w2_cp = fetch(w2, wv.at[0], 1)
    agg2_cp = fetch(agg2, agg.at[0], 2)
    blk_cp = fetch(blocks, blk, 3)
    pre_cp = fetch(pre1, pre, 4)
    w1_cp = fetch(w1, wv.at[1], 5)
    agg1_cp = fetch(agg1, agg.at[1], 6)

    pl.semaphore_wait(barrier, 6 + nz - 1 + ny - 1)

    sends = []

    def remote(src, dst, ssem, rsem, dev):
        return pltpu.make_async_remote_copy(
            src_ref=src, dst_ref=dst, send_sem=ssem, recv_sem=rsem, device_id=dev, device_id_type=MESH
        )

    def send(*a):
        cp = remote(*a)
        cp.start()
        sends.append(cp)

    def first_tile(c):
        base = (1 - core) * half if c < PARTS else core * half
        return base + (c % PARTS) * q

    def rows(c):
        return pl.ds(pl.multiple_of(first_tile(c) * tile, tile), ch)

    def gcopy(l, c, way, owner, dev):
        dst = gath.at[l, rows(c), cols(owner)]
        src = gp2.at[rows(c), :] if l == 0 and way < 2 else dst
        return src, dst, gsend.at[l, c, way], grecv.at[l, c, way], dev

    def send_own(l, c, way):
        send(*gcopy(l, c, way, x, right if way == 0 else left))

    def arrived(l, c, way):
        owner = lax.rem(x + (nx - 1, 1, 2)[way], nx)
        remote(*gcopy(l, c, way, owner, left)).wait_recv()

    def forward(l, c):
        if c % 2 == 0:
            arrived(l, c, 0)
            send(*gcopy(l, c, 2, left[1], right))
        else:
            arrived(l, c, 1)
            send(*gcopy(l, c, 2, right[1], left))

    def weigh(l, c):
        arrived(l, c, 1 if c % 2 == 0 else 0)
        arrived(l, c, 2)
        term = jnp.dot(aggt[l, c], gath[l, rows(c), :], preferred_element_type=F32)
        if c == 0:
            wacc[l] = term
        else:
            wacc[l] += term

    def multiply(l, c):
        def one(t, _):
            k = first_tile(c) + t
            g = gath[l, pl.ds(pl.multiple_of(k * tile, tile), tile), :]
            v = lax.dot_general(g, wv[l], (((1,), (1,)), ((), ())), preferred_element_type=F32).astype(BF)
            b = blk[pl.ds(k * bl, bl)].reshape(bl * tile, tile)
            prod[pl.ds(k * bl, bl)] = jnp.dot(b, v, preferred_element_type=F32).reshape(bl, tile, tile)
            return 0

        lax.fori_loop(0, q, one, 0, unroll=True)

    def transpose_agg(l):
        for c in range(chunks):
            aggt[l, c] = agg[l, rows(c), :].T

    def make_lists():
        lane = lax.broadcasted_iota(jnp.int32, (1, tile), 1)
        tg_cp.wait()

        def one(i, row):
            rel = tg[lax.rem(i, bl), i // bl] - (p - 2) * td
            off = lax.div(rel, td) - 2
            at = lax.rem(rel, td)
            turned = off * sig
            group = jnp.where(turned == -2, IF, jnp.where(turned == 2, OF, jnp.where(turned == -1, IN, ON)))
            to = jnp.where(off == 0, 4 * half + at, group * half + jnp.where(off < 0, at - half, at))
            key = to * nb + i
            slots[pl.ds(i, 1), :] = jnp.full((1, tile), to, jnp.int32)
            keys[pl.ds(i, 1), :] = jnp.full((1, tile), key, jnp.int32)
            return jnp.where(lane == i, key, row)

        row = lax.fori_loop(0, nb, one, jnp.full((1, tile), 1 << 20, jnp.int32))
        place = lax.broadcasted_iota(jnp.int32, (nb, tile), 1)
        block = lax.broadcasted_iota(jnp.int32, (nb, tile), 0)
        rank = jnp.sum((row < keys[...]).astype(jnp.int32), axis=1, keepdims=True)

        def add(mask, what):
            return jnp.sum(jnp.where(mask, what, 0), axis=0, keepdims=True)

        now, before = add(rank == place, slots[...]), add(rank == place - 1, slots[...])
        icols[0:1, :] = add(rank == place, block)
        icols[1:2, :] = jnp.maximum(add(slots[...] <= place, 1) - 1, 0)
        fcols[0:1, :] = jnp.where((now == before) & (lane > 0), 1.0, 0.0)
        fcols[1:2, :] = jnp.where(add(slots[...] == place, 1) > 0, 1.0, 0.0)
        icp = pltpu.make_async_copy(icols, ints, lsem.at[7])
        fcp = pltpu.make_async_copy(fcols, floats, lsem.at[8])
        icp.start()
        fcp.start()
        icp.wait()
        fcp.wait()

    def run_sums():
        def one(i, acc):
            acc = acc * floats[0, i] + prod[ints[0, i]]
            run[i] = acc
            return acc

        lax.fori_loop(0, nb, one, jnp.zeros((tile, tile), F32))

    def slot(s):
        return run[ints[1, s]] * floats[1, s]

    def ycopy(l, g, c, dev):
        at = pl.ds(c * yt, yt)
        return out.at[l, g, at], rec.at[l, g, at], ysend.at[l, g, c], yrecv.at[l, g, c], dev

    def emit(l, g, c, dev):
        def one(j, _):
            val = slot(g * half + c * yt + j)
            if g == ON:
                val = val + rec[l, H, c * yt + j].astype(F32)
            out[l, g, c * yt + j] = val.astype(BF)
            return 0

        if g == ON:
            remote(*ycopy(l, H, c, partner)).wait_recv()
        lax.fori_loop(0, yt, one, 0)
        send(*ycopy(l, g, c, dev))

    def spread(l):
        run_sums()
        for c in range(yc):
            emit(l, OF, c, far)
            emit(l, IF, c, partner)
        for c in range(yc):
            emit(l, IN, c, partner)
        for c in range(yc):
            emit(l, ON, c, near)

    def collect(l, c, put):
        groups = (B, N) if c < PARTS else (A,)
        cc = c % PARTS
        for g in groups:
            remote(*ycopy(l, g, cc, partner)).wait_recv()

        def one(j, _):
            k = first_tile(c) + j
            val = slot(4 * half + k)
            for g in groups:
                val = val + rec[l, g, cc * yt + j].astype(F32)
            put(k, val)
            return 0

        lax.fori_loop(0, q, one, 0)

    hc = wacc.shape[2] // 2

    def half_of(l, h):
        at = pl.ds(pl.multiple_of(h * hc, hc), hc)
        return (wacc[l, :, at] * scale).reshape(wzs.shape[1:])

    def c1copy(l):
        return w1s.at[l], w1r.at[l], csend.at[l], crecv.at[l], partner

    def weight1(l):
        w1s[l] = half_of(l, 1 - core).astype(BF)
        send(*c1copy(l))

    def others(n, me, make):
        def go(k, _):
            make(lax.rem(me + k, n)).start()
            return 0

        lax.fori_loop(1, n, go, 0)

    def all_recv(n, me, make):
        def go(k, _):
            make(lax.rem(me + k, n)).wait_recv()
            return 0

        lax.fori_loop(1, n, go, 0)

    def all_sent(n, me, make):
        def go(k, _):
            make(lax.rem(me + k, n)).wait_send()
            return 0

        lax.fori_loop(1, n, go, 0)

    side, at_a, at_b = nz, (z, y), (y, z)

    def adev(l, k):
        return zdev(k) if l == 0 else ydev(k)

    def bdev(l, k):
        return ydev(k) if l == 0 else zdev(k)

    def piece(k):
        n = wgs.shape[1]
        return pl.ds(pl.multiple_of(k * n, n), n)

    def zout(l):
        return lambda k: remote(wzs.at[l, k], wzr.at[l, at_a[l]], zsend.at[l, k], zrecv.at[l, at_a[l]], adev(l, k))

    def zin(l):
        return lambda k: remote(wzs.at[l, k], wzr.at[l, k], zsend.at[l, k], zrecv.at[l, k], adev(l, k))

    def yout(l):
        return lambda k: remote(wys.at[l], wyr.at[l, at_b[l]], vsend.at[l, k], vrecv.at[l, at_b[l]], bdev(l, k))

    def yin(l):
        return lambda k: remote(wys.at[l], wyr.at[l, k], vsend.at[l, k], vrecv.at[l, k], bdev(l, k))

    def gout(l):
        return lambda k: remote(wgs.at[l], wgr.at[l, piece(at_a[l])], tsend.at[l, k], trecv.at[l, at_a[l]], adev(l, k))

    def gin(l):
        return lambda k: remote(wgs.at[l], wgr.at[l, piece(k)], tsend.at[l, k], trecv.at[l, k], adev(l, k))

    def weight2(l):
        remote(*c1copy(l)).wait_recv()
        wzs[l] = (half_of(l, core) + w1r[l].astype(F32)).astype(BF)
        others(side, at_a[l], zout(l))

    def weight3(l):
        wzr[l, at_a[l]] = wzs[l, at_a[l]]
        all_recv(side, at_a[l], zin(l))
        total = wzr[l, 0].astype(F32)
        for k in range(1, nz):
            total = total + wzr[l, k].astype(F32)
        wys[l] = total.astype(BF)
        others(side, at_b[l], yout(l))

    def weight4(l):
        wyr[l, at_b[l]] = wys[l]
        all_recv(side, at_b[l], yin(l))
        total = wyr[l, 0].astype(F32)
        for k in range(1, ny):
            total = total + wyr[l, k].astype(F32)
        wgs[l] = total.astype(BF)
        others(side, at_a[l], gout(l))

    def c2copy(l):
        return wgr.at[l], wcr.at[l], c2send.at[l], c2recv.at[l], partner

    outs = []

    def put_weight(l, h, src, i):
        at = pl.ds(pl.multiple_of(h * hc, hc), hc)
        cp = pltpu.make_async_copy(src.at[l], gw.at[l, :, at], osem.at[l, i])
        cp.start()
        outs.append(cp)

    def weight5(l):
        wgr[l, piece(at_a[l])] = wgs[l]
        all_recv(side, at_a[l], gin(l))
        send(*c2copy(l))
        put_weight(l, core, wgr, 0)

    def weight6(l):
        remote(*c2copy(l)).wait_recv()
        put_weight(l, 1 - core, wcr, 1)

    evens, odds = list(range(0, chunks, 2)), list(range(1, chunks, 2))
    for c, d in zip(evens + odds, odds + evens):
        send_own(0, c, 0)
        send_own(0, d, 1)
    make_lists()
    agg2_cp.wait()
    transpose_agg(0)
    own_cp.wait()
    w2_cp.wait()
    blk_cp.wait()
    for c in range(chunks):
        forward(0, c)
    for c in range(chunks):
        weigh(0, c)
        multiply(0, c)
    weight1(0)
    spread(0)
    weight2(0)
    agg1_cp.wait()
    transpose_agg(1)
    pre_cp.wait()
    w1_cp.wait()

    def put_hidden(k, val):
        at = pl.ds(pl.multiple_of(k * tile, tile), tile)
        gath[1, at, cols(x)] = jnp.where(pre[at, :].astype(F32) > 0, val, 0.0).astype(BF)

    for c in range(chunks):
        collect(0, c, put_hidden)
        send_own(1, c, c % 2)
        send_own(1, c, 1 - c % 2)
    weight3(0)
    for c in range(chunks):
        forward(1, c)
    weight4(0)
    for c in range(chunks - 2):
        weigh(1, c)
        multiply(1, c)
    for c in range(chunks - 2, chunks):
        weigh(1, c)
    weight1(1)
    for c in range(chunks - 2, chunks):
        multiply(1, c)
    weight2(1)
    spread(1)
    weight3(1)
    weight5(0)

    def put_input(k, val):
        giv[k] = val.astype(BF)

    for c in range(chunks):
        collect(1, c, put_input)
        at = pl.ds(first_tile(c), q)
        cp = pltpu.make_async_copy(giv.at[at], gi.at[at], gisem.at[c])
        cp.start()
        outs.append(cp)
        if c == PARTS - 1:
            weight4(1)
    weight6(0)
    for cp in sends:
        cp.wait_send()
    sends.clear()
    for l in range(2):
        all_sent(side, at_a[l], zin(l))
        all_sent(side, at_b[l], yin(l))
    all_sent(side, at_a[0], gin(0))
    weight5(1)
    weight6(1)
    all_sent(side, at_a[1], gin(1))
    for cp in sends:
        cp.wait_send()
    for cp in outs:
        cp.wait()


def sizes(nd):
    chips = nd // 2
    nz = 1
    while nz * nz < chips:
        nz *= 2
    return nz, chips // nz


def shards(grad_pre2, aggregated2, weight2, pre1, aggregated1, weight1, blocks, targets):
    td, bl, tile, _ = blocks.shape
    nb, half = td * bl, td // 2
    nd = lax.axis_size("dom")
    rows, d = grad_pre2.shape[0], weight2.shape[1]
    nz, ny = sizes(nd)
    scale = 1.0 / math.sqrt(rows * nd)
    pr = tile // nz
    hbm = pl.BlockSpec(memory_space=pltpu.HBM)
    anywhere = pl.BlockSpec(memory_space=pl.ANY)
    dma = pltpu.SemaphoreType.DMA
    gw, gi = pl.pallas_call(
        functools.partial(kernel, nz, ny, td, scale),
        out_shape=(
            jax.ShapeDtypeStruct((2, tile, d), BF),
            jax.ShapeDtypeStruct((td, tile, tile), BF),
        ),
        in_specs=[hbm] * 8,
        out_specs=(anywhere, anywhere),
        scratch_shapes=[
            pltpu.VMEM((2, rows, d), BF),
            pltpu.VMEM((nb, tile, tile), BF),
            pltpu.VMEM((2, tile, d), BF),
            pltpu.VMEM((rows, tile), BF),
            pltpu.VMEM((2, rows, tile), BF),
            pltpu.VMEM((2, 2 * PARTS, tile, rows // (2 * PARTS)), BF),
            pltpu.VMEM((nb, tile, tile), F32),
            pltpu.VMEM((nb, tile, tile), F32),
            pltpu.VMEM((2, 4, half, tile, tile), BF),
            pltpu.VMEM((2, 4, half, tile, tile), BF),
            pltpu.VMEM((td, tile, tile), BF),
            pltpu.VMEM((2, tile, d), F32),
            pltpu.VMEM((nb, tile), jnp.int32),
            pltpu.VMEM((nb, tile), jnp.int32),
            pltpu.VMEM((8, tile), jnp.int32),
            pltpu.VMEM((8, tile), F32),
            pltpu.SMEM((bl, td), jnp.int32),
            pltpu.SMEM((8, tile), jnp.int32),
            pltpu.SMEM((8, tile), F32),
            pltpu.VMEM((2, nz, pr, d // 2), BF),
            pltpu.VMEM((2, nz, pr, d // 2), BF),
            pltpu.VMEM((2, nz, pr, d // 2), BF),
            pltpu.VMEM((2, nz, pr, d // 2), BF),
            pltpu.VMEM((2, pr, d // 2), BF),
            pltpu.VMEM((2, ny, pr, d // 2), BF),
            pltpu.VMEM((2, pr, d // 2), BF),
            pltpu.VMEM((2, tile, d // 2), BF),
            pltpu.VMEM((2, tile, d // 2), BF),
            dma((10,)),
            dma((2, 2)),
            dma((2 * PARTS,)),
            dma((2, 2 * PARTS, 3)),
            dma((2, 2 * PARTS, 3)),
            dma((2, 4, PARTS)),
            dma((2, 4, PARTS)),
            dma((2,)),
            dma((2,)),
            dma((2, nz)),
            dma((2, nz)),
            dma((2, ny)),
            dma((2, ny)),
            dma((2, nz)),
            dma((2, nz)),
            dma((2,)),
            dma((2,)),
        ],
        compiler_params=pltpu.CompilerParams(
            collective_id=0, has_side_effects=True, vmem_limit_bytes=40 * 1024 * 1024
        ),
    )(*(pltpu.with_memory_space_constraint(a, pltpu.HBM) for a in (grad_pre2, aggregated2, weight2, pre1, aggregated1, weight1, blocks.reshape(nb, tile, tile), targets.T)))
    return gw[0].astype(F32), gw[1].astype(F32), gi.reshape(rows, tile)


def solution(mesh):
    placed = (
        P("dom", "feat"),
        P("dom", "feat"),
        P("feat", None),
        P("dom", "feat"),
        P("dom", "feat"),
        P("feat", None),
        P("dom", None, None, None),
        P("dom", None),
    )
    return jax.shard_map(
        shards,
        mesh=mesh,
        in_specs=placed,
        out_specs=(P("feat", None), P("feat", None), P("dom", "feat")),
        check_vma=False,
    )
```

```python
import functools
import math

import jax
import jax.numpy as jnp
from jax import lax
from jax.experimental import pallas as pl
from jax.experimental.pallas import tpu as pltpu
from jax.sharding import PartitionSpec as P

MESH = pl.DeviceIdType.MESH
PARTS = 4
BF = jnp.bfloat16
F32 = jnp.float32
IF, OF, IN, ON = 0, 1, 2, 3
H, B, N, A = 0, 1, 2, 3


def kernel(
    nz, ny, td, scale,
    gp2, agg2, w2, pre1, agg1, w1, blocks, targets,
    gw, gi,
    gath, blk, wv, pre, agg, aggt, prod, run, out, rec, giv, wacc, keys, slots, icols, fcols, tg, ints, floats,
    w1s, w1r, wzs, wzr, wys, wyr, wgs, wgr, wcr,
    lsem, osem, gisem, gsend, grecv, ysend, yrecv, csend, crecv, zsend, zrecv, vsend, vrecv, tsend, trecv, c2send, c2recv, usend, urecv,
):
    nb, tile, _ = blocks.shape
    bl = nb // td
    half = td // 2
    q = half // PARTS
    ch = q * tile
    chunks = 2 * PARTS
    yc, yt = PARTS, q
    nx = lax.axis_size("feat")
    nd = lax.axis_size("dom")
    p = lax.axis_index("dom")
    x = lax.axis_index("feat")
    core = lax.rem(p, 2)
    y = lax.rem(p // 2, ny)
    z = p // (2 * ny)
    sig = 2 * core - 1

    def dom(step):
        return lax.rem(p + step + 2 * nd, nd)

    right = (p, lax.rem(x + 1, nx))
    left = (p, lax.rem(x + nx - 1, nx))
    partner, near, far, back = (dom(-sig), x), (dom(sig), x), (dom(2 * sig), x), (dom(-2 * sig), x)

    def zdev(k):
        return (k * (2 * ny) + y * 2 + core, x)

    def ydev(k):
        return (z * (2 * ny) + k * 2 + core, x)

    local = []

    def fetch(src, dst, i):
        cp = pltpu.make_async_copy(src, dst, lsem.at[i])
        cp.start()
        return cp

    def cols(k):
        return pl.ds(pl.multiple_of(k * tile, tile), tile)

    barrier = pltpu.get_barrier_semaphore()
    for dev in (left, right, partner, near, far, back):
        pl.semaphore_signal(barrier, inc=1, device_id=dev, device_id_type=MESH)

    def greet(k, _):
        pl.semaphore_signal(barrier, inc=1, device_id=zdev(lax.rem(z + k, nz)), device_id_type=MESH)
        return 0

    lax.fori_loop(1, nz, greet, 0)

    def greet_y(k, _):
        to = lax.rem(y + k, ny)
        pl.semaphore_signal(barrier, inc=1, device_id=ydev(to), device_id_type=MESH)
        pl.semaphore_signal(
            barrier, inc=1, device_id=(z * (2 * ny) + to * 2 + 1 - core, x), device_id_type=MESH
        )
        return 0

    lax.fori_loop(1, ny, greet_y, 0)

    tg_cp = fetch(targets, tg, 9)
    own_cp = fetch(gp2, gath.at[0, :, cols(x)], 0)
    w2_cp = fetch(w2, wv.at[0], 1)
    agg2_cp = fetch(agg2, agg.at[0], 2)
    blk_cp = fetch(blocks, blk, 3)
    pre_cp = fetch(pre1, pre, 4)
    w1_cp = fetch(w1, wv.at[1], 5)
    agg1_cp = fetch(agg1, agg.at[1], 6)

    pl.semaphore_wait(barrier, 6 + nz - 1 + 2 * (ny - 1))

    sends = []

    def remote(src, dst, ssem, rsem, dev):
        return pltpu.make_async_remote_copy(
            src_ref=src, dst_ref=dst, send_sem=ssem, recv_sem=rsem, device_id=dev, device_id_type=MESH
        )

    def send(*a):
        cp = remote(*a)
        cp.start()
        sends.append(cp)

    def first_tile(c):
        base = (1 - core) * half if c < PARTS else core * half
        return base + (c % PARTS) * q

    def rows(c):
        return pl.ds(pl.multiple_of(first_tile(c) * tile, tile), ch)

    def gcopy(l, c, way, owner, dev):
        dst = gath.at[l, rows(c), cols(owner)]
        src = gp2.at[rows(c), :] if l == 0 and way < 2 else dst
        return src, dst, gsend.at[l, c, way], grecv.at[l, c, way], dev

    def send_own(l, c, way):
        send(*gcopy(l, c, way, x, right if way == 0 else left))

    def arrived(l, c, way):
        owner = lax.rem(x + (nx - 1, 1, 2)[way], nx)
        remote(*gcopy(l, c, way, owner, left)).wait_recv()

    def forward(l, c):
        if c % 2 == 0:
            arrived(l, c, 0)
            send(*gcopy(l, c, 2, left[1], right))
        else:
            arrived(l, c, 1)
            send(*gcopy(l, c, 2, right[1], left))

    def weigh(l, c):
        arrived(l, c, 1 if c % 2 == 0 else 0)
        arrived(l, c, 2)
        term = jnp.dot(aggt[l, c], gath[l, rows(c), :], preferred_element_type=F32)
        if c == 0:
            wacc[l] = term
        else:
            wacc[l] += term

    def multiply(l, c):
        def one(t, _):
            k = first_tile(c) + t
            g = gath[l, pl.ds(pl.multiple_of(k * tile, tile), tile), :]
            v = lax.dot_general(g, wv[l], (((1,), (1,)), ((), ())), preferred_element_type=F32).astype(BF)
            b = blk[pl.ds(k * bl, bl)].reshape(bl * tile, tile)
            prod[pl.ds(k * bl, bl)] = jnp.dot(b, v, preferred_element_type=F32).reshape(bl, tile, tile)
            return 0

        lax.fori_loop(0, q, one, 0, unroll=True)

    def transpose_agg(l):
        for c in range(chunks):
            aggt[l, c] = agg[l, rows(c), :].T

    def make_lists():
        lane = lax.broadcasted_iota(jnp.int32, (1, tile), 1)
        tg_cp.wait()

        def one(i, row):
            rel = tg[lax.rem(i, bl), i // bl] - (p - 2) * td
            off = lax.div(rel, td) - 2
            at = lax.rem(rel, td)
            turned = off * sig
            group = jnp.where(turned == -2, IF, jnp.where(turned == 2, OF, jnp.where(turned == -1, IN, ON)))
            to = jnp.where(off == 0, 4 * half + at, group * half + jnp.where(off < 0, at - half, at))
            key = to * nb + i
            slots[pl.ds(i, 1), :] = jnp.full((1, tile), to, jnp.int32)
            keys[pl.ds(i, 1), :] = jnp.full((1, tile), key, jnp.int32)
            return jnp.where(lane == i, key, row)

        row = lax.fori_loop(0, nb, one, jnp.full((1, tile), 1 << 20, jnp.int32))
        place = lax.broadcasted_iota(jnp.int32, (nb, tile), 1)
        block = lax.broadcasted_iota(jnp.int32, (nb, tile), 0)
        rank = jnp.sum((row < keys[...]).astype(jnp.int32), axis=1, keepdims=True)

        def add(mask, what):
            return jnp.sum(jnp.where(mask, what, 0), axis=0, keepdims=True)

        now, before = add(rank == place, slots[...]), add(rank == place - 1, slots[...])
        icols[0:1, :] = add(rank == place, block)
        icols[1:2, :] = jnp.maximum(add(slots[...] <= place, 1) - 1, 0)
        fcols[0:1, :] = jnp.where((now == before) & (lane > 0), 1.0, 0.0)
        fcols[1:2, :] = jnp.where(add(slots[...] == place, 1) > 0, 1.0, 0.0)
        icp = pltpu.make_async_copy(icols, ints, lsem.at[7])
        fcp = pltpu.make_async_copy(fcols, floats, lsem.at[8])
        icp.start()
        fcp.start()
        icp.wait()
        fcp.wait()

    def run_sums():
        def one(i, acc):
            acc = acc * floats[0, i] + prod[ints[0, i]]
            run[i] = acc
            return acc

        lax.fori_loop(0, nb, one, jnp.zeros((tile, tile), F32))

    def slot(s):
        return run[ints[1, s]] * floats[1, s]

    def ycopy(l, g, c, dev):
        at = pl.ds(c * yt, yt)
        return out.at[l, g, at], rec.at[l, g, at], ysend.at[l, g, c], yrecv.at[l, g, c], dev

    def emit(l, g, c, dev):
        def one(j, _):
            val = slot(g * half + c * yt + j)
            if g == ON:
                val = val + rec[l, H, c * yt + j].astype(F32)
            out[l, g, c * yt + j] = val.astype(BF)
            return 0

        if g == ON:
            remote(*ycopy(l, H, c, partner)).wait_recv()
        lax.fori_loop(0, yt, one, 0)
        send(*ycopy(l, g, c, dev))

    def spread(l):
        run_sums()
        for c in range(yc):
            emit(l, OF, c, far)
            emit(l, IF, c, partner)
        for c in range(yc):
            emit(l, IN, c, partner)
        for c in range(yc):
            emit(l, ON, c, near)

    def collect(l, c, put):
        groups = (B, N) if c < PARTS else (A,)
        cc = c % PARTS
        for g in groups:
            remote(*ycopy(l, g, cc, partner)).wait_recv()

        def one(j, _):
            k = first_tile(c) + j
            val = slot(4 * half + k)
            for g in groups:
                val = val + rec[l, g, cc * yt + j].astype(F32)
            put(k, val)
            return 0

        lax.fori_loop(0, q, one, 0)

    hc = wacc.shape[2] // 2

    def half_of(l, h):
        at = pl.ds(pl.multiple_of(h * hc, hc), hc)
        return (wacc[l, :, at] * scale).reshape(wzs.shape[1:])

    def c1copy(l):
        return w1s.at[l], w1r.at[l], csend.at[l], crecv.at[l], partner

    def weight1(l):
        w1s[l] = half_of(l, 1 - core).astype(BF)
        send(*c1copy(l))

    def others(n, me, make):
        def go(k, _):
            make(lax.rem(me + k, n)).start()
            return 0

        lax.fori_loop(1, n, go, 0)

    def all_recv(n, me, make):
        def go(k, _):
            make(lax.rem(me + k, n)).wait_recv()
            return 0

        lax.fori_loop(1, n, go, 0)

    def all_sent(n, me, make):
        def go(k, _):
            make(lax.rem(me + k, n)).wait_send()
            return 0

        lax.fori_loop(1, n, go, 0)

    side, at_a, at_b = nz, (z, y), (y, z)

    def adev(l, k):
        return zdev(k) if l == 0 else ydev(k)

    def bdev(l, k):
        return ydev(k) if l == 0 else zdev(k)

    def piece(k):
        n = wgs.shape[1]
        return pl.ds(pl.multiple_of(k * n, n), n)

    def zout(l):
        return lambda k: remote(wzs.at[l, k], wzr.at[l, at_a[l]], zsend.at[l, k], zrecv.at[l, at_a[l]], adev(l, k))

    def zin(l):
        return lambda k: remote(wzs.at[l, k], wzr.at[l, k], zsend.at[l, k], zrecv.at[l, k], adev(l, k))

    def yout(l):
        return lambda k: remote(wys.at[l], wyr.at[l, at_b[l]], vsend.at[l, k], vrecv.at[l, at_b[l]], bdev(l, k))

    def yin(l):
        return lambda k: remote(wys.at[l], wyr.at[l, k], vsend.at[l, k], vrecv.at[l, k], bdev(l, k))

    def gout(l):
        return lambda k: remote(wgs.at[l], wgr.at[l, piece(at_a[l])], tsend.at[l, k], trecv.at[l, at_a[l]], adev(l, k))

    def gin(l):
        return lambda k: remote(wgs.at[l], wgr.at[l, piece(k)], tsend.at[l, k], trecv.at[l, k], adev(l, k))

    def weight2(l):
        remote(*c1copy(l)).wait_recv()
        wzs[l] = (half_of(l, core) + w1r[l].astype(F32)).astype(BF)
        others(side, at_a[l], zout(l))

    def weight3(l):
        wzr[l, at_a[l]] = wzs[l, at_a[l]]
        all_recv(side, at_a[l], zin(l))
        total = wzr[l, 0].astype(F32)
        for k in range(1, nz):
            total = total + wzr[l, k].astype(F32)
        wys[l] = total.astype(BF)
        others(side, at_b[l], yout(l))

    def weight4(l):
        wyr[l, at_b[l]] = wys[l]
        all_recv(side, at_b[l], yin(l))
        total = wyr[l, 0].astype(F32)
        for k in range(1, ny):
            total = total + wyr[l, k].astype(F32)
        wgs[l] = total.astype(BF)
        others(side, at_a[l], gout(l))
        if l == 1:
            across(y).start()
            others(side, y, across)

    def yboth(k):
        return (z * (2 * ny) + k * 2 + 1 - core, x)

    def across(k):
        return remote(wgs.at[1], wcr.at[1, piece(y)], usend.at[k], urecv.at[y], yboth(k))

    def across_in(k):
        return remote(wgs.at[1], wcr.at[1, piece(k)], usend.at[k], urecv.at[k], yboth(k))

    def c2copy(l):
        return wgr.at[l], wcr.at[l], c2send.at[l], c2recv.at[l], partner

    outs = []

    def put_weight(l, h, src, i):
        at = pl.ds(pl.multiple_of(h * hc, hc), hc)
        cp = pltpu.make_async_copy(src.at[l], gw.at[l, :, at], osem.at[l, i])
        cp.start()
        outs.append(cp)

    def weight5(l):
        wgr[l, piece(at_a[l])] = wgs[l]
        all_recv(side, at_a[l], gin(l))
        if l == 0:
            send(*c2copy(l))
        put_weight(l, core, wgr, 0)

    def weight6(l):
        if l == 0:
            remote(*c2copy(l)).wait_recv()
        else:
            across_in(y).wait_recv()
            all_recv(side, y, across_in)
        put_weight(l, 1 - core, wcr, 1)

    evens, odds = list(range(0, chunks, 2)), list(range(1, chunks, 2))
    for c, d in zip(evens + odds, odds + evens):
        send_own(0, c, 0)
        send_own(0, d, 1)
    make_lists()
    agg2_cp.wait()
    transpose_agg(0)
    own_cp.wait()
    w2_cp.wait()
    blk_cp.wait()
    for c in range(chunks):
        forward(0, c)
    for c in range(chunks):
        weigh(0, c)
        multiply(0, c)
    weight1(0)
    spread(0)
    weight2(0)
    agg1_cp.wait()
    transpose_agg(1)
    pre_cp.wait()
    w1_cp.wait()

    def put_hidden(k, val):
        at = pl.ds(pl.multiple_of(k * tile, tile), tile)
        gath[1, at, cols(x)] = jnp.where(pre[at, :].astype(F32) > 0, val, 0.0).astype(BF)

    for c in range(chunks):
        collect(0, c, put_hidden)
        send_own(1, c, c % 2)
        send_own(1, c, 1 - c % 2)
    weight3(0)
    for c in range(chunks):
        forward(1, c)
    weight4(0)
    for c in range(chunks - 2):
        weigh(1, c)
        multiply(1, c)
    for c in range(chunks - 2, chunks):
        weigh(1, c)
    weight1(1)
    for c in range(chunks - 2, chunks):
        multiply(1, c)
    weight2(1)
    spread(1)
    weight3(1)
    weight5(0)

    def put_input(k, val):
        giv[k] = val.astype(BF)

    for c in range(chunks):
        collect(1, c, put_input)
        at = pl.ds(first_tile(c), q)
        cp = pltpu.make_async_copy(giv.at[at], gi.at[at], gisem.at[c])
        cp.start()
        outs.append(cp)
        if c == PARTS - 1:
            weight4(1)
    weight6(0)
    for cp in sends:
        cp.wait_send()
    sends.clear()
    for l in range(2):
        all_sent(side, at_a[l], zin(l))
        all_sent(side, at_b[l], yin(l))
    all_sent(side, at_a[0], gin(0))
    weight5(1)
    weight6(1)
    all_sent(side, at_a[1], gin(1))
    across_in(y).wait_send()
    all_sent(side, y, across_in)
    for cp in sends:
        cp.wait_send()
    for cp in outs:
        cp.wait()


def sizes(nd):
    chips = nd // 2
    nz = 1
    while nz * nz < chips:
        nz *= 2
    return nz, chips // nz


def shards(grad_pre2, aggregated2, weight2, pre1, aggregated1, weight1, blocks, targets):
    td, bl, tile, _ = blocks.shape
    nb, half = td * bl, td // 2
    nd = lax.axis_size("dom")
    rows, d = grad_pre2.shape[0], weight2.shape[1]
    nz, ny = sizes(nd)
    scale = 1.0 / math.sqrt(rows * nd)
    pr = tile // nz
    hbm = pl.BlockSpec(memory_space=pltpu.HBM)
    anywhere = pl.BlockSpec(memory_space=pl.ANY)
    dma = pltpu.SemaphoreType.DMA
    gw, gi = pl.pallas_call(
        functools.partial(kernel, nz, ny, td, scale),
        out_shape=(
            jax.ShapeDtypeStruct((2, tile, d), BF),
            jax.ShapeDtypeStruct((td, tile, tile), BF),
        ),
        in_specs=[hbm] * 8,
        out_specs=(anywhere, anywhere),
        scratch_shapes=[
            pltpu.VMEM((2, rows, d), BF),
            pltpu.VMEM((nb, tile, tile), BF),
            pltpu.VMEM((2, tile, d), BF),
            pltpu.VMEM((rows, tile), BF),
            pltpu.VMEM((2, rows, tile), BF),
            pltpu.VMEM((2, 2 * PARTS, tile, rows // (2 * PARTS)), BF),
            pltpu.VMEM((nb, tile, tile), F32),
            pltpu.VMEM((nb, tile, tile), F32),
            pltpu.VMEM((2, 4, half, tile, tile), BF),
            pltpu.VMEM((2, 4, half, tile, tile), BF),
            pltpu.VMEM((td, tile, tile), BF),
            pltpu.VMEM((2, tile, d), F32),
            pltpu.VMEM((nb, tile), jnp.int32),
            pltpu.VMEM((nb, tile), jnp.int32),
            pltpu.VMEM((8, tile), jnp.int32),
            pltpu.VMEM((8, tile), F32),
            pltpu.SMEM((bl, td), jnp.int32),
            pltpu.SMEM((8, tile), jnp.int32),
            pltpu.SMEM((8, tile), F32),
            pltpu.VMEM((2, nz, pr, d // 2), BF),
            pltpu.VMEM((2, nz, pr, d // 2), BF),
            pltpu.VMEM((2, nz, pr, d // 2), BF),
            pltpu.VMEM((2, nz, pr, d // 2), BF),
            pltpu.VMEM((2, pr, d // 2), BF),
            pltpu.VMEM((2, ny, pr, d // 2), BF),
            pltpu.VMEM((2, pr, d // 2), BF),
            pltpu.VMEM((2, tile, d // 2), BF),
            pltpu.VMEM((2, tile, d // 2), BF),
            dma((10,)),
            dma((2, 2)),
            dma((2 * PARTS,)),
            dma((2, 2 * PARTS, 3)),
            dma((2, 2 * PARTS, 3)),
            dma((2, 4, PARTS)),
            dma((2, 4, PARTS)),
            dma((2,)),
            dma((2,)),
            dma((2, nz)),
            dma((2, nz)),
            dma((2, ny)),
            dma((2, ny)),
            dma((2, nz)),
            dma((2, nz)),
            dma((2,)),
            dma((2,)),
            dma((ny,)),
            dma((ny,)),
        ],
        compiler_params=pltpu.CompilerParams(
            collective_id=0, has_side_effects=True, vmem_limit_bytes=40 * 1024 * 1024
        ),
    )(*(pltpu.with_memory_space_constraint(a, pltpu.HBM) for a in (grad_pre2, aggregated2, weight2, pre1, aggregated1, weight1, blocks.reshape(nb, tile, tile), targets.T)))
    return gw[0].astype(F32), gw[1].astype(F32), gi.reshape(rows, tile)


def solution(mesh):
    placed = (
        P("dom", "feat"),
        P("dom", "feat"),
        P("feat", None),
        P("dom", "feat"),
        P("dom", "feat"),
        P("feat", None),
        P("dom", None, None, None),
        P("dom", None),
    )
    return jax.shard_map(
        shards,
        mesh=mesh,
        in_specs=placed,
        out_specs=(P("feat", None), P("feat", None), P("dom", "feat")),
        check_vma=False,
    )
```
